128 devices in a mesh: gx: 8 (over y, core), gy: 16 (over x, z).
Axes of the slice: x: 4, y: 4, z: 4, core: 2. Of those that a mesh axis runs over, the one named last changes fastest.
Arguments:
- tokens_in: bfloat16 [16384, 1024], P(('gx', 'gy')), may hold values from -64 to 64
- dest_slot: int32 [16384], P(('gx', 'gy')), may hold values from 0 to 16383, as said below
- w_query: bfloat16 [1024, 1024], replicated, may hold values from -1.5 to 1.5
- w_key: bfloat16 [1024, 1024], replicated, may hold values from -0.75 to 0.75
- w_value: bfloat16 [1024, 1024], replicated, may hold values from -0.1875 to 0.1875
- surrogate: bfloat16 [1024], replicated, may hold values from -4 to 4
- gain_cluster: float32 [1024], replicated, may hold values from 0.25 to 1.75
- gain_summary: float32 [1024], replicated, may hold values from 0.25 to 1.75
- w_out: bfloat16 [1024, 1024], replicated, may hold values from -0.1875 to 0.1875
Outputs:
- layer_out: bfloat16 [16384, 1024], P(('gx', 'gy'))
The draws below stay inside these ranges and needn't reach their ends.
Inputs may be any that keep to these rules, and one draw needn't show every extreme that they name: dest_slot is a permutation of the 16384 slots, so every cluster has exactly 128 members. Slot s lies on device s // 128, which thus holds exactly 128 slots. Of the 128 tokens of one device at most 2 have slots on any one device, and in every draw, the device at mesh position (gx, gy) has exactly 2 tokens with slots on the device at ((gx + 4) % 8, gy).
All inputs are finite; a program needn't handle non-finite values.
Results may differ from the reference program's by a relative error of at most 0.011.
Values may be sent and summed in bfloat16 or wider, within the bound.
A program may use at most 64 MiB of HBM per device.

```python
import math
import jax
import jax.numpy as jnp
from jax import lax

D = 1024
HEADS = 16
HEAD_DIM = 64
CSIZE = 128
TOK_DEV = 128
SHARDS = 128
TOKENS = 16384
CLUSTERS = 128
MEAN_PAIR = 1


def clipped_normal(key, salt, shape):
    return jnp.clip(jax.random.normal(jax.random.fold_in(key, salt), shape, jnp.float32), -4.0, 4.0)


def query_matrix(key):
    return clipped_normal(key, 11, (D, D)) * (1.0 / math.sqrt(D))


def key_matrix(key):
    independent = clipped_normal(key, 12, (D, D)) * (1.0 / math.sqrt(D))
    return independent


def draw_w_query(key, part):
    return (3.0 * query_matrix(key)).astype(jnp.bfloat16)


def draw_w_key(key, part):
    return key_matrix(key).astype(jnp.bfloat16)


def draw_surrogate(key, part):
    noise_part = clipped_normal(key, 14, (HEADS, HEAD_DIM))
    values = noise_part
    return values.reshape(D).astype(jnp.bfloat16)


def draw_tokens_in(key, part):
    base_key = jax.random.fold_in(key, 21)
    values = jnp.clip(jax.random.normal(base_key, (TOKENS, D), jnp.float32), -4.0, 4.0)
    return values.astype(jnp.bfloat16)


def shuffled(key_batch, length):

    def single(one_key):
        return jax.random.permutation(one_key, length)
    return jax.vmap(single)(key_batch).astype(jnp.int32)


def force_shift(shifts, index, wanted):
    where_now = jnp.argmax((shifts == wanted).astype(jnp.int32)).astype(jnp.int32)
    previous = shifts[index]
    return shifts.at[where_now].set(previous).at[index].set(wanted)


def draw_dest_slot(key, part):
    key_one, key_two, key_three, key_four = jax.random.split(key, 4)
    half_count = SHARDS // 2
    offsets = jax.random.randint(key_one, (half_count,), 0, MEAN_PAIR + 1).astype(jnp.int32)
    offsets = offsets.at[0].set(MEAN_PAIR)
    pair_counts = jnp.concatenate([MEAN_PAIR + offsets, MEAN_PAIR - offsets])
    shifts = jax.random.permutation(key_two, SHARDS).astype(jnp.int32)
    shifts = force_shift(shifts, 0, SHARDS // 2)
    shifts = force_shift(shifts, 1, 1)
    shifts = force_shift(shifts, 2, SHARDS - 1)
    group_end = jnp.cumsum(pair_counts).astype(jnp.int32)
    group_start = group_end - pair_counts
    send_order = shuffled(jax.random.split(key_three, SHARDS), TOK_DEV)
    group = jnp.searchsorted(group_end, send_order, side='right').astype(jnp.int32)
    rank_in = send_order - group_start[group]
    sender = jnp.arange(SHARDS, dtype=jnp.int32)[:, None]
    owner_dev = (sender + shifts[group]) % SHARDS
    recv_order = shuffled(jax.random.split(key_four, SHARDS), TOK_DEV)
    local_slot = recv_order[owner_dev, group_start[group] + rank_in]
    return (owner_dev * TOK_DEV + local_slot).reshape(TOKENS).astype(jnp.int32)


def centred(rng, extent, scale, bound, kind=jnp.bfloat16):
    values = jax.random.normal(rng, extent, jnp.float32) * scale
    return jnp.minimum(jnp.maximum(values, -bound), bound).astype(kind)


def setup_inputs(seed: int = 0) -> dict:
    seeds = jax.random.split(jax.random.key(seed), 10)
    tokens_in = draw_tokens_in(jax.random.fold_in(seeds[9], 71), 0)
    dest_slot = draw_dest_slot(jax.random.fold_in(seeds[9], 71), 0)
    w_query = draw_w_query(jax.random.fold_in(seeds[9], 71), 0)
    w_key = draw_w_key(jax.random.fold_in(seeds[9], 71), 0)
    w_value = centred(seeds[4], (D, D), D ** -0.5, 0.1875)
    surrogate = draw_surrogate(jax.random.fold_in(seeds[9], 71), 0)
    gain_cluster = jnp.clip(1.0 + 0.15 * jax.random.normal(seeds[6], (D,), jnp.float32), 0.25, 1.75)
    gain_summary = jnp.clip(1.0 + 0.15 * jax.random.normal(seeds[7], (D,), jnp.float32), 0.25, 1.75)
    w_out = centred(seeds[8], (D, D), D ** -0.5, 0.1875)
    return {"tokens_in": tokens_in, "dest_slot": dest_slot, "w_query": w_query, "w_key": w_key, "w_value": w_value, "surrogate": surrogate, "gain_cluster": gain_cluster, "gain_summary": gain_summary, "w_out": w_out}


def rms_scale(values, gain_vec):
    mean_sq = lax.optimization_barrier(jnp.mean(values * values, axis=-1, keepdims=True))
    return values * lax.rsqrt(mean_sq + 1e-06) * gain_vec

def project(row_data, weight):
    return jnp.dot(row_data, weight, preferred_element_type=jnp.float32).astype(jnp.bfloat16)

def rounded(values):
    return lax.optimization_barrier(values.astype(jnp.bfloat16)).astype(jnp.float32)

def cluster_part(q_block, k_block, v_block, surrogate, gain_cluster):
    groups = q_block.shape[0] // CSIZE
    scaling = 1.0 / math.sqrt(HEAD_DIM)
    query_heads = q_block.astype(jnp.float32).reshape(groups, CSIZE, HEADS, HEAD_DIM)
    key_heads = k_block.astype(jnp.float32).reshape(groups, CSIZE, HEADS, HEAD_DIM)
    value_heads = v_block.astype(jnp.float32).reshape(groups, CSIZE, HEADS, HEAD_DIM)
    scores = jnp.einsum('cihd,cjhd->chij', query_heads, key_heads) * scaling
    attn_probs = rounded(jax.nn.softmax(scores, axis=-1))
    attended = jnp.einsum('chij,cjhd->cihd', attn_probs, value_heads).reshape(groups * CSIZE, D)
    branch = rms_scale(attended, gain_cluster).astype(jnp.bfloat16)
    anchor = surrogate.astype(jnp.float32).reshape(HEADS, HEAD_DIM)
    logits = jnp.einsum('cihd,hd->chi', key_heads, anchor) * scaling
    pooled = rounded(jax.nn.softmax(logits, axis=-1))
    key_sum = jnp.einsum('chi,cihd->chd', pooled, key_heads)
    value_summary = jnp.einsum('chi,cihd->chd', pooled, value_heads).astype(jnp.bfloat16)
    mean_sq = lax.optimization_barrier(jnp.mean(key_sum * key_sum, axis=-1, keepdims=True))
    key_summary = (key_sum * lax.rsqrt(mean_sq + 1e-06)).astype(jnp.bfloat16)
    return (branch, key_summary.reshape(groups, D), value_summary.reshape(groups, D))

def reference(tokens_in, dest_slot, w_query, w_key, w_value, surrogate, gain_cluster, gain_summary, w_out):
    query = project(tokens_in, w_query)
    key_rows = project(tokens_in, w_key)
    value_rows = project(tokens_in, w_value)
    inverse = jnp.zeros((TOKENS,), jnp.int32).at[dest_slot].set(jnp.arange(TOKENS, dtype=jnp.int32))

    def per_device(blocks):
        return cluster_part(blocks[0], blocks[1], blocks[2], surrogate, gain_cluster)
    shaped = (query[inverse].reshape(SHARDS, TOK_DEV, D), key_rows[inverse].reshape(SHARDS, TOK_DEV, D), value_rows[inverse].reshape(SHARDS, TOK_DEV, D))
    branch_slot, key_summary, value_summary = lax.map(per_device, shaped)
    cluster_out = branch_slot.reshape(TOKENS, D)[dest_slot]
    scaling = 1.0 / math.sqrt(HEAD_DIM)
    key_heads = key_summary.reshape(CLUSTERS, HEADS, HEAD_DIM).astype(jnp.float32)
    value_heads = value_summary.reshape(CLUSTERS, HEADS, HEAD_DIM).astype(jnp.float32)

    def summary_part(q_block):
        query_heads = q_block.astype(jnp.float32).reshape(TOK_DEV, HEADS, HEAD_DIM)
        logits = jnp.einsum('thd,chd->htc', query_heads, key_heads) * scaling
        top_val = lax.optimization_barrier(jnp.max(logits, axis=-1, keepdims=True))
        raised = jnp.exp(logits - top_val)
        denom_sum = lax.optimization_barrier(jnp.sum(raised, axis=-1))
        weighted = jnp.einsum('htc,chd->thd', rounded(raised), value_heads)
        summary_att = (weighted / denom_sum.T[:, :, None]).reshape(TOK_DEV, D)
        return rms_scale(summary_att, gain_summary)
    summary_out = lax.map(summary_part, query.reshape(SHARDS, TOK_DEV, D)).reshape(TOKENS, D)
    mixture = (cluster_out.astype(jnp.float32) + summary_out).astype(jnp.bfloat16)
    return jnp.dot(mixture, w_out, preferred_element_type=jnp.float32).astype(jnp.bfloat16)
```

```python
import functools
import math

import jax
import jax.numpy as jnp
from jax import lax
from jax.experimental import pallas as pl
from jax.experimental.pallas import tpu as pltpu
from jax.sharding import PartitionSpec as P

MESH = pl.DeviceIdType.MESH
F32, BF16 = jnp.float32, jnp.bfloat16
GX, GY = 8, 16
N = GX * GY
T = 128
D = 1024
HEADS, HD = 16, 64
PAIRS = D // 128
CAP = 2
ROWS = N * CAP
PAD = 128.0
MARK = 1024.0
EXP2_SCALE = math.log2(math.e) / math.sqrt(HD)


def iota(shape, dim):
    return lax.broadcasted_iota(jnp.int32, shape, dim).astype(F32)


def dot(a, b):
    return jnp.dot(a, b, preferred_element_type=F32)


def dot_nt(a, b):
    return lax.dot_general(a, b, (((1,), (1,)), ((), ())), preferred_element_type=F32)


def dot_tn(a, b):
    return lax.dot_general(a, b, (((0,), (0,)), ((), ())), preferred_element_type=F32)


def attend_pair(q_tile, k_tile, v_tile, low):
    zero = jnp.zeros_like(q_tile)
    q_two = jnp.concatenate([jnp.where(low, q_tile, zero), jnp.where(low, zero, q_tile)], axis=0)
    scores = dot_nt(q_two, k_tile)
    top = jnp.max(scores, axis=1, keepdims=True)
    raised = jnp.exp2((scores - top) * EXP2_SCALE)
    total = 1.0 / jnp.sum(raised, axis=1, keepdims=True)
    raised = raised.astype(BF16)
    both = jnp.concatenate([raised[:T], raised[T:]], axis=1)
    v_two = jnp.concatenate([jnp.where(low, v_tile, zero), jnp.where(low, zero, v_tile)], axis=0)
    return dot(both, v_two) * jnp.where(low, total[:T], total[T:])


def kernel(
    x_ref, slot_ref, surr_ref, gain_c_ref, gain_s_ref, wq_hbm, wk_hbm, wv_hbm, wo_hbm,
    out_ref,
    wq, wk, wv, wo, stage, rows, send_buf, recv_buf, back_buf, home_buf, sum_buf, sums_buf, att, q_loc,
    w_sem, fwd_send, fwd_recv, sum_send, sum_recv, back_send, back_recv, row_sem,
):
    gx, gy = lax.axis_index("gx"), lax.axis_index("gy")
    me = gx * GY + gy

    loads = [
        pltpu.make_async_copy(src, dst, w_sem.at[i])
        for i, (src, dst) in enumerate(((wq_hbm, wq), (wk_hbm, wk), (wv_hbm, wv), (wo_hbm, wo)))
    ]
    for load in loads:
        load.start()

    with jax.named_scope("barrier_a"):
        barrier = pltpu.get_barrier_semaphore()
        for i in range(1, GX):
            pl.semaphore_signal(barrier, inc=1, device_id=(lax.rem(gx + i, GX), gy), device_id_type=MESH)
        for i in range(1, GY):
            pl.semaphore_signal(barrier, inc=1, device_id=(gx, lax.rem(gy + i, GY)), device_id_type=MESH)

    with jax.named_scope("pack"):
        owner_row = (slot_ref[...] >> 7).astype(F32)
        sub, lane = iota((T, T), 0), iota((T, T), 1)
        owner_wide = jnp.broadcast_to(owner_row, (T, T))
        owner_col = jnp.sum(jnp.where(sub == lane, owner_wide, 0.0), axis=1, keepdims=True)
        same = (owner_col == owner_wide).astype(F32)
        place_row = owner_row * CAP + jnp.sum(jnp.where(sub < lane, same, 0.0), axis=0, keepdims=True)
        place_col = owner_col * CAP + jnp.sum(jnp.where(lane < sub, same, 0.0), axis=1, keepdims=True)
        pick = (iota((ROWS, T), 0) == place_row).astype(F32)
        filled = jnp.sum(pick, axis=1, keepdims=True) > 0.5
        pick = pick.astype(BF16)
        for j in range(PAIRS):
            part = dot(pick, x_ref[:, j * 128 : (j + 1) * 128])
            stage[pl.ds(j, ROWS, stride=8), :] = jnp.where(filled, part, PAD)
        send_buf[...] = stage[...].astype(BF16).reshape(N, 16, 128)

    with jax.named_scope("barrier_b"):
        pl.semaphore_wait(barrier, GX + GY - 2)
        for i in range(1, GX):
            pl.semaphore_signal(row_sem, inc=1, device_id=(lax.rem(gx + i, GX), gy), device_id_type=MESH)
        pl.semaphore_wait(row_sem, GX - 1)

    def to_all(src_of, dst, send_sem, recv_sem):
        def send(i, carry):
            tx = lax.rem(gx + i // GY, GX)
            ty = lax.rem(gy + lax.rem(i, GY), GY)
            pltpu.make_async_remote_copy(
                src_ref=src_of(tx * GY + ty),
                dst_ref=dst.at[me],
                send_sem=send_sem,
                recv_sem=recv_sem,
                device_id=(tx, ty),
                device_id_type=MESH,
            ).start()
            return carry

        lax.fori_loop(1, N, send, 0)

    def wait_all(buf, sem):
        some = buf.at[pl.ds(0, N - 1)]
        pltpu.make_async_copy(some, some, sem).wait()

    with jax.named_scope("send_tokens"):
        to_all(lambda d: send_buf.at[d], recv_buf, fwd_send, fwd_recv)
    recv_buf[pl.ds(me, 1)] = send_buf[pl.ds(me, 1)]

    with jax.named_scope("local_query"):
        loads[0].wait()
        q_loc[...] = dot(x_ref[...], wq[...]).astype(BF16)

    def unpack(buf):
        stage[...] = buf[...].astype(F32).reshape(ROWS * 8, 128)
        for j in range(PAIRS):
            rows[:, j * 128 : (j + 1) * 128] = stage[pl.ds(j, ROWS, stride=8), :].astype(BF16)

    with jax.named_scope("wait_tokens"):
        wait_all(recv_buf, fwd_recv)
    with jax.named_scope("unpack"):
        unpack(recv_buf)
        real = (rows[:, :128].astype(F32) < 100.0).astype(BF16)
        r_sub, r_lane = iota((ROWS, ROWS), 0), iota((ROWS, ROWS), 1)
        mark = jnp.where(r_sub == r_lane, -MARK, 0.0)
        rank_row = dot_tn(real, (mark + (r_sub < r_lane).astype(F32)).astype(BF16))
        rank_col = dot((mark + (r_lane < r_sub).astype(F32)).astype(BF16), real)
        gather = (rank_row == iota((T, ROWS), 0) - MARK).astype(BF16)
        scatter = (rank_col == iota((ROWS, T), 1) - MARK).astype(BF16)
        members = dot(gather, rows[...]).astype(BF16)

    with jax.named_scope("key_value"):
        loads[1].wait()
        key = dot(members, wk[...]).astype(BF16)
        loads[2].wait()
        value = dot(members, wv[...]).astype(BF16)

    with jax.named_scope("summary"):
        own = lax.broadcasted_iota(jnp.int32, (HEADS, D), 1) // HD == lax.broadcasted_iota(
            jnp.int32, (HEADS, D), 0
        )
        anchor = jnp.where(own, jnp.broadcast_to(surr_ref[...].astype(F32), (HEADS, D)), 0.0).astype(BF16)
        logits = dot_nt(anchor, key)
        raised = jnp.exp2((logits - jnp.max(logits, axis=1, keepdims=True)) * EXP2_SCALE)
        pooled = (raised / jnp.sum(raised, axis=1, keepdims=True)).astype(BF16)
        key_sum = jnp.where(own, dot(pooled, key), 0.0)
        key_sum = key_sum * lax.rsqrt(jnp.sum(key_sum * key_sum, axis=1, keepdims=True) / HD + 1e-6)
        key_sum = jnp.sum(key_sum, axis=0, keepdims=True)
        value_sum = jnp.sum(jnp.where(own, dot(pooled, value), 0.0), axis=0, keepdims=True)
        for j in range(PAIRS):
            stage[j : j + 1, :] = key_sum[:, j * 128 : (j + 1) * 128]
            stage[8 + j : 9 + j, :] = value_sum[:, j * 128 : (j + 1) * 128]
        sum_buf[...] = stage[:16, :].astype(BF16)
    with jax.named_scope("send_summary"):
        to_all(lambda d: sum_buf, sums_buf, sum_send, sum_recv)
    sums_buf[pl.ds(me, 1)] = sum_buf[...][None]

    low = lax.broadcasted_iota(jnp.int32, (T, 128), 1) < HD

    with jax.named_scope("query"):
        query = dot(members, wq[...]).astype(BF16)
    with jax.named_scope("attend"):
        square = jnp.zeros((T, 128), F32)
        for j in range(PAIRS):
            at = slice(j * 128, (j + 1) * 128)
            got = attend_pair(query[:, at], key[:, at], value[:, at], low)
            square = square + got * got
            att[:, at] = got
        scale = lax.rsqrt(jnp.sum(square, axis=1, keepdims=True) / D + 1e-6)
        branch = (att[...] * scale * gain_c_ref[...]).astype(BF16)
    with jax.named_scope("pack_back"):
        for j in range(PAIRS):
            stage[pl.ds(j, ROWS, stride=8), :] = dot(scatter, branch[:, j * 128 : (j + 1) * 128])
        back_buf[...] = stage[...].astype(BF16).reshape(N, 16, 128)
    with jax.named_scope("send_back"):
        to_all(lambda d: back_buf.at[d], home_buf, back_send, back_recv)
    home_buf[pl.ds(me, 1)] = back_buf[pl.ds(me, 1)]

    with jax.named_scope("wait_summary"):
        wait_all(sums_buf, sum_recv)
    with jax.named_scope("attend_summary"):
        stage[...] = sums_buf[...].astype(F32).reshape(N * 16, 128)
        square = jnp.zeros((T, 128), F32)
        for j in range(PAIRS):
            at = slice(j * 128, (j + 1) * 128)
            got = attend_pair(
                q_loc[:, at],
                stage[pl.ds(j, N, stride=16), :].astype(BF16),
                stage[pl.ds(8 + j, N, stride=16), :].astype(BF16),
                low,
            )
            square = square + got * got
            att[:, at] = got
        scale = lax.rsqrt(jnp.sum(square, axis=1, keepdims=True) / D + 1e-6)
        att[...] = att[...] * scale * gain_s_ref[...]

    with jax.named_scope("wait_back"):
        wait_all(home_buf, back_recv)
    with jax.named_scope("mix_out"):
        unpack(home_buf)
        pick_back = (iota((T, ROWS), 1) == place_col).astype(BF16)
        mixture = (dot(pick_back, rows[...]) + att[...]).astype(BF16)
        loads[3].wait()
        out_ref[...] = dot(mixture, wo[...]).astype(BF16)

    with jax.named_scope("drain"):
        wait_all(send_buf, fwd_send)
        wait_all(sums_buf, sum_send)
        wait_all(back_buf, back_send)


def body(
    tokens_in, dest_slot, w_query, w_key, w_value, surrogate, gain_cluster, gain_summary, w_out
):
    vmem, hbm = pl.BlockSpec(memory_space=pltpu.VMEM), pl.BlockSpec(memory_space=pl.ANY)
    tiles = pltpu.VMEM((N, 16, 128), BF16)
    weight = pltpu.VMEM((D, D), BF16)
    dma = pltpu.SemaphoreType.DMA
    return pl.pallas_call(
        kernel,
        out_shape=jax.ShapeDtypeStruct((T, D), BF16),
        in_specs=[vmem] * 5 + [hbm] * 4,
        out_specs=vmem,
        scratch_shapes=[weight] * 4
        + [
            pltpu.VMEM((ROWS * 8, 128), F32),
            pltpu.VMEM((ROWS, D), BF16),
            tiles, tiles, tiles, tiles,
            pltpu.VMEM((16, 128), BF16),
            tiles,
            pltpu.VMEM((T, D), F32),
            pltpu.VMEM((T, D), BF16),
            dma((4,)), dma, dma, dma, dma, dma, dma,
            pltpu.SemaphoreType.REGULAR,
        ],
        compiler_params=pltpu.CompilerParams(
            collective_id=0, has_side_effects=True, vmem_limit_bytes=60 * 2**20
        ),
    )(
        tokens_in,
        dest_slot.reshape(1, T),
        surrogate.reshape(1, D),
        gain_cluster.reshape(1, D),
        gain_summary.reshape(1, D),
        w_query, w_key, w_value, w_out,
    )


def solution(mesh):
    in_specs = (P(("gx", "gy"), None), P(("gx", "gy")), P(), P(), P(), P(), P(), P(), P())
    out_specs = P(("gx", "gy"), None)
    return jax.shard_map(body, mesh=mesh, in_specs=in_specs, out_specs=out_specs, check_vma=False)
```

```python
import functools
import math

import jax
import jax.numpy as jnp
from jax import lax
from jax.experimental import pallas as pl
from jax.experimental.pallas import tpu as pltpu
from jax.sharding import PartitionSpec as P

MESH = pl.DeviceIdType.MESH
F32, BF16 = jnp.float32, jnp.bfloat16
GX, GY = 8, 16
N = GX * GY
CHIPS = N // 2
T = 128
D = 1024
HEADS, HD = 16, 64
PAIRS = D // 128
CAP = 2
ROWS = N * CAP
PAD = 128.0
MARK = 1024.0
EXP2_SCALE = math.log2(math.e) / math.sqrt(HD)


def iota(shape, dim):
    return lax.broadcasted_iota(jnp.int32, shape, dim).astype(F32)


def dot(a, b):
    return jnp.dot(a, b, preferred_element_type=F32)


def dot_nt(a, b):
    return lax.dot_general(a, b, (((1,), (1,)), ((), ())), preferred_element_type=F32)


def dot_tn(a, b):
    return lax.dot_general(a, b, (((0,), (0,)), ((), ())), preferred_element_type=F32)


def attend_pair(q_tile, k_tile, v_tile, low):
    zero = jnp.zeros_like(q_tile)
    q_two = jnp.concatenate([jnp.where(low, q_tile, zero), jnp.where(low, zero, q_tile)], axis=0)
    scores = dot_nt(q_two, k_tile)
    top = jnp.max(scores, axis=1, keepdims=True)
    raised = jnp.exp2((scores - top) * EXP2_SCALE)
    total = 1.0 / jnp.sum(raised, axis=1, keepdims=True)
    raised = raised.astype(BF16)
    both = jnp.concatenate([raised[:T], raised[T:]], axis=1)
    v_two = jnp.concatenate([jnp.where(low, v_tile, zero), jnp.where(low, zero, v_tile)], axis=0)
    return dot(both, v_two) * jnp.where(low, total[:T], total[T:])


def kernel(
    x_hbm, slot_hbm, surr_hbm, gain_c_hbm, gain_s_hbm, wq_hbm, wk_hbm, wv_hbm, wo_hbm,
    out_ref,
    x_ref, slot_ref, surr_ref, gain_c_ref, gain_s_ref, wq, wk, wv, wo, stage, rows, send_buf, recv_buf, back_buf, home_buf, sum_buf, sums_buf, att, q_loc,
    x_sem, w_sem, fwd_send, fwd_recv, sum_send, sum_recv, pass_send, pass_recv, back_send, back_recv, row_sem,
):
    gx, gy = lax.axis_index("gx"), lax.axis_index("gy")
    me = gx * GY + gy

    y, core = gx // 2, lax.rem(gx, 2)
    firsts = [
        pltpu.make_async_copy(src, dst, x_sem.at[i])
        for i, (src, dst) in enumerate(((slot_hbm, slot_ref), (x_hbm, x_ref)))
    ]
    loads = [
        pltpu.make_async_copy(src, dst, w_sem.at[i])
        for i, (src, dst) in enumerate(
            (
                (wq_hbm, wq), (wk_hbm, wk), (wv_hbm, wv), (wo_hbm, wo),
                (surr_hbm, surr_ref), (gain_c_hbm, gain_c_ref), (gain_s_hbm, gain_s_ref),
            )
        )
    ]
    for load in firsts:
        load.start()

    with jax.named_scope("barrier_a"):
        barrier = pltpu.get_barrier_semaphore()
        for i in range(1, GX):
            pl.semaphore_signal(barrier, inc=1, device_id=(lax.rem(gx + i, GX), gy), device_id_type=MESH)
        for i in range(1, GY):
            pl.semaphore_signal(barrier, inc=1, device_id=(gx, lax.rem(gy + i, GY)), device_id_type=MESH)

    with jax.named_scope("pack"):
        for load in firsts:
            load.wait()
        for load in loads:
            load.start()
        owner_row = (slot_ref[...] >> 7).astype(F32)
        sub, lane = iota((T, T), 0), iota((T, T), 1)
        owner_wide = jnp.broadcast_to(owner_row, (T, T))
        owner_col = jnp.sum(jnp.where(sub == lane, owner_wide, 0.0), axis=1, keepdims=True)
        same = (owner_col == owner_wide).astype(F32)
        place_row = owner_row * CAP + jnp.sum(jnp.where(sub < lane, same, 0.0), axis=0, keepdims=True)
        place_col = owner_col * CAP + jnp.sum(jnp.where(lane < sub, same, 0.0), axis=1, keepdims=True)
        pick = (iota((ROWS, T), 0) == place_row).astype(F32)
        filled = jnp.sum(pick, axis=1, keepdims=True) > 0.5
        pick = pick.astype(BF16)
        for j in range(PAIRS):
            part = dot(pick, x_ref[:, j * 128 : (j + 1) * 128])
            stage[pl.ds(j, ROWS, stride=8), :] = jnp.where(filled, part, PAD)
        send_buf[...] = stage[...].astype(BF16).reshape(N, 16, 128)

    with jax.named_scope("barrier_b"):
        pl.semaphore_wait(barrier, GX + GY - 2)
        for i in range(1, GX):
            pl.semaphore_signal(row_sem, inc=1, device_id=(lax.rem(gx + i, GX), gy), device_id_type=MESH)
        pl.semaphore_wait(row_sem, GX - 1)

    def to_all(src_of, dst, send_sem, recv_sem):
        def send(i, carry):
            tx = lax.rem(gx + i // GY, GX)
            ty = lax.rem(gy + lax.rem(i, GY), GY)
            pltpu.make_async_remote_copy(
                src_ref=src_of(tx * GY + ty),
                dst_ref=dst.at[me],
                send_sem=send_sem,
                recv_sem=recv_sem,
                device_id=(tx, ty),
                device_id_type=MESH,
            ).start()
            return carry

        lax.fori_loop(1, N, send, 0)

    def wait_for(buf, count, sem):
        some = buf.at[pl.ds(0, count)]
        pltpu.make_async_copy(some, some, sem).wait()

    def wait_all(buf, sem):
        wait_for(buf, N - 1, sem)

    with jax.named_scope("send_tokens"):
        to_all(lambda d: send_buf.at[d], recv_buf, fwd_send, fwd_recv)
    recv_buf[pl.ds(me, 1)] = send_buf[pl.ds(me, 1)]

    with jax.named_scope("local_query"):
        loads[0].wait()
        q_loc[...] = dot(x_ref[...], wq[...]).astype(BF16)

    def unpack(buf):
        stage[...] = buf[...].astype(F32).reshape(ROWS * 8, 128)
        for j in range(PAIRS):
            rows[:, j * 128 : (j + 1) * 128] = stage[pl.ds(j, ROWS, stride=8), :].astype(BF16)

    with jax.named_scope("wait_tokens"):
        wait_all(recv_buf, fwd_recv)
    with jax.named_scope("unpack"):
        unpack(recv_buf)
        real = (rows[:, :128].astype(F32) < 100.0).astype(BF16)
        r_sub, r_lane = iota((ROWS, ROWS), 0), iota((ROWS, ROWS), 1)
        mark = jnp.where(r_sub == r_lane, -MARK, 0.0)
        rank_row = dot_tn(real, (mark + (r_sub < r_lane).astype(F32)).astype(BF16))
        rank_col = dot((mark + (r_lane < r_sub).astype(F32)).astype(BF16), real)
        gather = (rank_row == iota((T, ROWS), 0) - MARK).astype(BF16)
        scatter = (rank_col == iota((ROWS, T), 1) - MARK).astype(BF16)
        members = dot(gather, rows[...]).astype(BF16)

    with jax.named_scope("key_value"):
        loads[1].wait()
        key = dot(members, wk[...]).astype(BF16)
        loads[2].wait()
        value = dot(members, wv[...]).astype(BF16)

    with jax.named_scope("summary"):
        own = lax.broadcasted_iota(jnp.int32, (HEADS, D), 1) // HD == lax.broadcasted_iota(
            jnp.int32, (HEADS, D), 0
        )
        loads[4].wait()
        surr = surr_ref[...].astype(F32)
        surr = jnp.concatenate([surr[j : j + 1] for j in range(PAIRS)], axis=1)
        anchor = jnp.where(own, jnp.broadcast_to(surr, (HEADS, D)), 0.0).astype(BF16)
        logits = dot_nt(anchor, key)
        raised = jnp.exp2((logits - jnp.max(logits, axis=1, keepdims=True)) * EXP2_SCALE)
        pooled = (raised / jnp.sum(raised, axis=1, keepdims=True)).astype(BF16)
        key_sum = jnp.where(own, dot(pooled, key), 0.0)
        key_sum = key_sum * lax.rsqrt(jnp.sum(key_sum * key_sum, axis=1, keepdims=True) / HD + 1e-6)
        key_sum = jnp.sum(key_sum, axis=0, keepdims=True)
        value_sum = jnp.sum(jnp.where(own, dot(pooled, value), 0.0), axis=0, keepdims=True)
        for j in range(PAIRS):
            stage[j : j + 1, :] = key_sum[:, j * 128 : (j + 1) * 128]
            stage[8 + j : 9 + j, :] = value_sum[:, j * 128 : (j + 1) * 128]
        sum_buf[...] = stage[:16, :].astype(BF16)
    with jax.named_scope("send_summary"):
        mine = core * CHIPS + y * GY + gy
        for dy in range(4):

            def send(i, carry, dy=dy):
                tx, ty = lax.rem(gx + 2 * dy, GX), lax.rem(gy + i, GY)
                pltpu.make_async_remote_copy(
                    src_ref=sum_buf,
                    dst_ref=sums_buf.at[mine],
                    send_sem=sum_send,
                    recv_sem=sum_recv.at[dy],
                    device_id=(tx, ty),
                    device_id_type=MESH,
                ).start()
                return carry

            lax.fori_loop(1 if dy == 0 else 0, GY, send, 0)
        sums_buf[pl.ds(mine, 1)] = sum_buf[...][None]

    low = lax.broadcasted_iota(jnp.int32, (T, 128), 1) < HD

    with jax.named_scope("query"):
        query = dot(members, wq[...]).astype(BF16)
    with jax.named_scope("attend"):
        square = jnp.zeros((T, 128), F32)
        for j in range(PAIRS):
            at = slice(j * 128, (j + 1) * 128)
            got = attend_pair(query[:, at], key[:, at], value[:, at], low)
            square = square + got * got
            att[:, at] = got
        scale = lax.rsqrt(jnp.sum(square, axis=1, keepdims=True) / D + 1e-6)
        loads[5].wait()
        branch = (att[...] * scale * gain_c_ref[...]).astype(BF16)
    with jax.named_scope("pack_back"):
        for j in range(PAIRS):
            stage[pl.ds(j, ROWS, stride=8), :] = dot(scatter, branch[:, j * 128 : (j + 1) * 128])
        back_buf[...] = stage[...].astype(BF16).reshape(N, 16, 128)
    with jax.named_scope("send_back"):
        to_all(lambda d: back_buf.at[d], home_buf, back_send, back_recv)
    home_buf[pl.ds(me, 1)] = back_buf[pl.ds(me, 1)]

    with jax.named_scope("pass_summary"):
        passes = []
        for dy in range(4):
            wait_for(sums_buf, GY - 1 if dy == 0 else GY, sum_recv.at[dy])
            block = sums_buf.at[pl.ds(core * CHIPS + lax.rem(y + 4 - dy, 4) * GY, GY)]
            passes.append(
                pltpu.make_async_remote_copy(
                    src_ref=block,
                    dst_ref=block,
                    send_sem=pass_send.at[dy],
                    recv_sem=pass_recv.at[dy],
                    device_id=(gx + 1 - 2 * core, gy),
                    device_id_type=MESH,
                )
            )
            passes[-1].start()
        for one in passes:
            one.wait()
    with jax.named_scope("attend_summary"):
        stage[...] = sums_buf[...].astype(F32).reshape(N * 16, 128)
        square = jnp.zeros((T, 128), F32)
        for j in range(PAIRS):
            at = slice(j * 128, (j + 1) * 128)
            got = attend_pair(
                q_loc[:, at],
                stage[pl.ds(j, N, stride=16), :].astype(BF16),
                stage[pl.ds(8 + j, N, stride=16), :].astype(BF16),
                low,
            )
            square = square + got * got
            att[:, at] = got
        scale = lax.rsqrt(jnp.sum(square, axis=1, keepdims=True) / D + 1e-6)
        loads[6].wait()
        att[...] = att[...] * scale * gain_s_ref[...]

    with jax.named_scope("wait_back"):
        wait_all(home_buf, back_recv)
    with jax.named_scope("mix_out"):
        unpack(home_buf)
        pick_back = (iota((T, ROWS), 1) == place_col).astype(BF16)
        mixture = (dot(pick_back, rows[...]) + att[...]).astype(BF16)
        loads[3].wait()
        out_ref[...] = dot(mixture, wo[...]).astype(BF16)

    with jax.named_scope("drain"):
        wait_all(send_buf, fwd_send)
        wait_for(sums_buf, CHIPS - 1, sum_send)
        wait_all(back_buf, back_send)


def body(
    tokens_in, dest_slot, w_query, w_key, w_value, surrogate, gain_cluster, gain_summary, w_out
):
    vmem, hbm = pl.BlockSpec(memory_space=pltpu.VMEM), pl.BlockSpec(memory_space=pl.ANY)
    tiles = pltpu.VMEM((N, 16, 128), BF16)
    weight = pltpu.VMEM((D, D), BF16)
    dma = pltpu.SemaphoreType.DMA
    return pl.pallas_call(
        kernel,
        out_shape=jax.ShapeDtypeStruct((T, D), BF16),
        in_specs=[hbm] * 9,
        out_specs=vmem,
        scratch_shapes=[
            pltpu.VMEM((T, D), BF16),
            pltpu.VMEM((1, T), jnp.int32),
            pltpu.VMEM((PAIRS, 128), BF16),
            pltpu.VMEM((1, D), F32),
            pltpu.VMEM((1, D), F32),
        ]
        + [weight] * 4
        + [
            pltpu.VMEM((ROWS * 8, 128), F32),
            pltpu.VMEM((ROWS, D), BF16),
            tiles, tiles, tiles, tiles,
            pltpu.VMEM((16, 128), BF16),
            tiles,
            pltpu.VMEM((T, D), F32),
            pltpu.VMEM((T, D), BF16),
            dma((2,)), dma((7,)), dma, dma, dma, dma((4,)), dma((4,)), dma((4,)), dma, dma,
            pltpu.SemaphoreType.REGULAR,
        ],
        compiler_params=pltpu.CompilerParams(
            collective_id=0, has_side_effects=True, vmem_limit_bytes=60 * 2**20
        ),
    )(
        tokens_in,
        dest_slot.reshape(1, T),
        surrogate.reshape(PAIRS, 128),
        gain_cluster.reshape(1, D),
        gain_summary.reshape(1, D),
        w_query, w_key, w_value, w_out,
    )


def solution(mesh):
    in_specs = (P(("gx", "gy"), None), P(("gx", "gy")), P(), P(), P(), P(), P(), P(), P())
    out_specs = P(("gx", "gy"), None)
    return jax.shard_map(body, mesh=mesh, in_specs=in_specs, out_specs=out_specs, check_vma=False)
```

```python
import functools
import math

import jax
import jax.numpy as jnp
from jax import lax
from jax.experimental import pallas as pl
from jax.experimental.pallas import tpu as pltpu
from jax.sharding import PartitionSpec as P

MESH = pl.DeviceIdType.MESH
F32, BF16 = jnp.float32, jnp.bfloat16
GX, GY = 8, 16
N = GX * GY
CHIPS = N // 2
T = 128
D = 1024
HEADS, HD = 16, 64
PAIRS = D // 128
CAP = 2
ROWS = N * CAP
PAD = 128.0
MARK = 1024.0
EXP2_SCALE = math.log2(math.e) / math.sqrt(HD)


def iota(shape, dim):
    return lax.broadcasted_iota(jnp.int32, shape, dim).astype(F32)


def dot(a, b):
    return jnp.dot(a, b, preferred_element_type=F32)


def dot_nt(a, b):
    return lax.dot_general(a, b, (((1,), (1,)), ((), ())), preferred_element_type=F32)


def dot_tn(a, b):
    return lax.dot_general(a, b, (((0,), (0,)), ((), ())), preferred_element_type=F32)


def attend_pair(q_tile, k_tile, v_tile, low):
    zero = jnp.zeros_like(q_tile)
    q_two = jnp.concatenate([jnp.where(low, q_tile, zero), jnp.where(low, zero, q_tile)], axis=0)
    scores = dot_nt(q_two, k_tile)
    top = jnp.max(scores, axis=1, keepdims=True)
    raised = jnp.exp2((scores - top) * EXP2_SCALE)
    total = 1.0 / jnp.sum(raised, axis=1, keepdims=True)
    raised = raised.astype(BF16)
    both = jnp.concatenate([raised[:T], raised[T:]], axis=1)
    v_two = jnp.concatenate([jnp.where(low, v_tile, zero), jnp.where(low, zero, v_tile)], axis=0)
    return dot(both, v_two) * jnp.where(low, total[:T], total[T:])


def kernel(
    x_hbm, slot_hbm, surr_hbm, gain_c_hbm, gain_s_hbm, wq_hbm, wk_hbm, wv_hbm,
    out_ref,
    x_ref, slot_ref, surr_ref, gain_c_ref, gain_s_ref, wq, wk, wv, stage, rows, send_buf, recv_buf, back_buf, home_buf, sum_buf, sums_buf, att, q_loc,
    x_sem, w_sem, fwd_send, fwd_recv, sum_send, sum_recv, pass_send, pass_recv, back_send, back_recv, row_sem,
):
    gx, gy = lax.axis_index("gx"), lax.axis_index("gy")
    me = gx * GY + gy

    y, core = gx // 2, lax.rem(gx, 2)
    firsts = [
        pltpu.make_async_copy(src, dst, x_sem.at[i])
        for i, (src, dst) in enumerate(((slot_hbm, slot_ref), (x_hbm, x_ref)))
    ]
    loads = [
        pltpu.make_async_copy(src, dst, w_sem.at[i])
        for i, (src, dst) in enumerate(
            (
                (wq_hbm, wq), (wk_hbm, wk), (wv_hbm, wv),
                (surr_hbm, surr_ref), (gain_c_hbm, gain_c_ref), (gain_s_hbm, gain_s_ref),
            )
        )
    ]
    for load in firsts:
        load.start()

    with jax.named_scope("barrier_a"):
        barrier = pltpu.get_barrier_semaphore()
        for i in range(1, GX):
            pl.semaphore_signal(barrier, inc=1, device_id=(lax.rem(gx + i, GX), gy), device_id_type=MESH)
        for i in range(1, GY):
            pl.semaphore_signal(barrier, inc=1, device_id=(gx, lax.rem(gy + i, GY)), device_id_type=MESH)

    with jax.named_scope("pack"):
        for load in firsts:
            load.wait()
        for load in loads:
            load.start()
        owner_row = (slot_ref[...] >> 7).astype(F32)
        sub, lane = iota((T, T), 0), iota((T, T), 1)
        owner_wide = jnp.broadcast_to(owner_row, (T, T))
        owner_col = jnp.sum(jnp.where(sub == lane, owner_wide, 0.0), axis=1, keepdims=True)
        same = (owner_col == owner_wide).astype(F32)
        place_row = owner_row * CAP + jnp.sum(jnp.where(sub < lane, same, 0.0), axis=0, keepdims=True)
        place_col = owner_col * CAP + jnp.sum(jnp.where(lane < sub, same, 0.0), axis=1, keepdims=True)
        pick = (iota((ROWS, T), 0) == place_row).astype(F32)
        filled = jnp.sum(pick, axis=1, keepdims=True) > 0.5
        pick = pick.astype(BF16)
        for j in range(PAIRS):
            part = dot(pick, x_ref[:, j * 128 : (j + 1) * 128])
            stage[pl.ds(j, ROWS, stride=8), :] = jnp.where(filled, part, PAD)
        send_buf[...] = stage[...].astype(BF16).reshape(N, 16, 128)

    with jax.named_scope("barrier_b"):
        pl.semaphore_wait(barrier, GX + GY - 2)
        for i in range(1, GX):
            pl.semaphore_signal(row_sem, inc=1, device_id=(lax.rem(gx + i, GX), gy), device_id_type=MESH)
        pl.semaphore_wait(row_sem, GX - 1)

    def to_all(src_of, dst, send_sem, recv_sem):
        def send(i, carry):
            tx = lax.rem(gx + i // GY, GX)
            ty = lax.rem(gy + lax.rem(i, GY), GY)
            pltpu.make_async_remote_copy(
                src_ref=src_of(tx * GY + ty),
                dst_ref=dst.at[me],
                send_sem=send_sem,
                recv_sem=recv_sem,
                device_id=(tx, ty),
                device_id_type=MESH,
            ).start()
            return carry

        lax.fori_loop(1, N, send, 0)

    def wait_for(buf, count, sem):
        some = buf.at[pl.ds(0, count)]
        pltpu.make_async_copy(some, some, sem).wait()

    def wait_all(buf, sem):
        wait_for(buf, N - 1, sem)

    with jax.named_scope("send_tokens"):
        to_all(lambda d: send_buf.at[d], recv_buf, fwd_send, fwd_recv)
    recv_buf[pl.ds(me, 1)] = send_buf[pl.ds(me, 1)]

    with jax.named_scope("local_query"):
        loads[0].wait()
        q_loc[...] = dot(x_ref[...], wq[...]).astype(BF16)

    def unpack(buf):
        stage[...] = buf[...].astype(F32).reshape(ROWS * 8, 128)
        for j in range(PAIRS):
            rows[:, j * 128 : (j + 1) * 128] = stage[pl.ds(j, ROWS, stride=8), :].astype(BF16)

    with jax.named_scope("wait_tokens"):
        wait_all(recv_buf, fwd_recv)
    with jax.named_scope("unpack"):
        unpack(recv_buf)
        real = (rows[:, :128].astype(F32) < 100.0).astype(BF16)
        r_sub, r_lane = iota((ROWS, ROWS), 0), iota((ROWS, ROWS), 1)
        mark = jnp.where(r_sub == r_lane, -MARK, 0.0)
        rank_row = dot_tn(real, (mark + (r_sub < r_lane).astype(F32)).astype(BF16))
        rank_col = dot((mark + (r_lane < r_sub).astype(F32)).astype(BF16), real)
        gather = (rank_row == iota((T, ROWS), 0) - MARK).astype(BF16)
        scatter = (rank_col == iota((ROWS, T), 1) - MARK).astype(BF16)
        members = dot(gather, rows[...]).astype(BF16)

    with jax.named_scope("key_value"):
        loads[1].wait()
        key = dot(members, wk[...]).astype(BF16)
        loads[2].wait()
        value = dot(members, wv[...]).astype(BF16)

    with jax.named_scope("summary"):
        own = lax.broadcasted_iota(jnp.int32, (HEADS, D), 1) // HD == lax.broadcasted_iota(
            jnp.int32, (HEADS, D), 0
        )
        loads[3].wait()
        surr = surr_ref[...].astype(F32)
        surr = jnp.concatenate([surr[j : j + 1] for j in range(PAIRS)], axis=1)
        anchor = jnp.where(own, jnp.broadcast_to(surr, (HEADS, D)), 0.0).astype(BF16)
        logits = dot_nt(anchor, key)
        raised = jnp.exp2((logits - jnp.max(logits, axis=1, keepdims=True)) * EXP2_SCALE)
        pooled = (raised / jnp.sum(raised, axis=1, keepdims=True)).astype(BF16)
        key_sum = jnp.where(own, dot(pooled, key), 0.0)
        key_sum = key_sum * lax.rsqrt(jnp.sum(key_sum * key_sum, axis=1, keepdims=True) / HD + 1e-6)
        key_sum = jnp.sum(key_sum, axis=0, keepdims=True)
        value_sum = jnp.sum(jnp.where(own, dot(pooled, value), 0.0), axis=0, keepdims=True)
        for j in range(PAIRS):
            stage[j : j + 1, :] = key_sum[:, j * 128 : (j + 1) * 128]
            stage[8 + j : 9 + j, :] = value_sum[:, j * 128 : (j + 1) * 128]
        sum_buf[...] = stage[:16, :].astype(BF16)
    with jax.named_scope("send_summary"):
        mine = core * CHIPS + y * GY + gy
        for dy in range(4):

            def send(i, carry, dy=dy):
                tx, ty = lax.rem(gx + 2 * dy, GX), lax.rem(gy + i, GY)
                pltpu.make_async_remote_copy(
                    src_ref=sum_buf,
                    dst_ref=sums_buf.at[mine],
                    send_sem=sum_send,
                    recv_sem=sum_recv.at[dy],
                    device_id=(tx, ty),
                    device_id_type=MESH,
                ).start()
                return carry

            lax.fori_loop(1 if dy == 0 else 0, GY, send, 0)
        sums_buf[pl.ds(mine, 1)] = sum_buf[...][None]

    low = lax.broadcasted_iota(jnp.int32, (T, 128), 1) < HD

    with jax.named_scope("query"):
        query = dot(members, wq[...]).astype(BF16)
    with jax.named_scope("attend"):
        square = jnp.zeros((T, 128), F32)
        for j in range(PAIRS):
            at = slice(j * 128, (j + 1) * 128)
            got = attend_pair(query[:, at], key[:, at], value[:, at], low)
            square = square + got * got
            att[:, at] = got
        scale = lax.rsqrt(jnp.sum(square, axis=1, keepdims=True) / D + 1e-6)
        loads[4].wait()
        branch = (att[...] * scale * gain_c_ref[...]).astype(BF16)
    with jax.named_scope("pack_back"):
        for j in range(PAIRS):
            stage[pl.ds(j, ROWS, stride=8), :] = dot(scatter, branch[:, j * 128 : (j + 1) * 128])
        back_buf[...] = stage[...].astype(BF16).reshape(N, 16, 128)
    with jax.named_scope("send_back"):
        to_all(lambda d: back_buf.at[d], home_buf, back_send, back_recv)
    home_buf[pl.ds(me, 1)] = back_buf[pl.ds(me, 1)]

    with jax.named_scope("pass_summary"):
        passes = []
        for dy in range(4):
            wait_for(sums_buf, GY - 1 if dy == 0 else GY, sum_recv.at[dy])
            block = sums_buf.at[pl.ds(core * CHIPS + lax.rem(y + 4 - dy, 4) * GY, GY)]
            passes.append(
                pltpu.make_async_remote_copy(
                    src_ref=block,
                    dst_ref=block,
                    send_sem=pass_send.at[dy],
                    recv_sem=pass_recv.at[dy],
                    device_id=(gx + 1 - 2 * core, gy),
                    device_id_type=MESH,
                )
            )
            passes[-1].start()
        for one in passes:
            one.wait()
    with jax.named_scope("attend_summary"):
        stage[...] = sums_buf[...].astype(F32).reshape(N * 16, 128)
        square = jnp.zeros((T, 128), F32)
        for j in range(PAIRS):
            at = slice(j * 128, (j + 1) * 128)
            got = attend_pair(
                q_loc[:, at],
                stage[pl.ds(j, N, stride=16), :].astype(BF16),
                stage[pl.ds(8 + j, N, stride=16), :].astype(BF16),
                low,
            )
            square = square + got * got
            att[:, at] = got
        scale = lax.rsqrt(jnp.sum(square, axis=1, keepdims=True) / D + 1e-6)
        loads[5].wait()
        att[...] = att[...] * scale * gain_s_ref[...]

    with jax.named_scope("wait_back"):
        wait_all(home_buf, back_recv)
    with jax.named_scope("mix_out"):
        unpack(home_buf)
        pick_back = (iota((T, ROWS), 1) == place_col).astype(BF16)
        mixture = (dot(pick_back, rows[...]) + att[...]).astype(BF16)
        out_ref[...] = mixture

    with jax.named_scope("drain"):
        wait_all(send_buf, fwd_send)
        wait_for(sums_buf, CHIPS - 1, sum_send)
        wait_all(back_buf, back_send)


def body(
    tokens_in, dest_slot, w_query, w_key, w_value, surrogate, gain_cluster, gain_summary, w_out
):
    vmem, hbm = pl.BlockSpec(memory_space=pltpu.VMEM), pl.BlockSpec(memory_space=pl.ANY)
    tiles = pltpu.VMEM((N, 16, 128), BF16)
    weight = pltpu.VMEM((D, D), BF16)
    dma = pltpu.SemaphoreType.DMA
    mixture = pl.pallas_call(
        kernel,
        out_shape=jax.ShapeDtypeStruct((T, D), BF16),
        in_specs=[hbm] * 8,
        out_specs=vmem,
        scratch_shapes=[
            pltpu.VMEM((T, D), BF16),
            pltpu.VMEM((1, T), jnp.int32),
            pltpu.VMEM((PAIRS, 128), BF16),
            pltpu.VMEM((1, D), F32),
            pltpu.VMEM((1, D), F32),
        ]
        + [weight] * 3
        + [
            pltpu.VMEM((ROWS * 8, 128), F32),
            pltpu.VMEM((ROWS, D), BF16),
            tiles, tiles, tiles, tiles,
            pltpu.VMEM((16, 128), BF16),
            tiles,
            pltpu.VMEM((T, D), F32),
            pltpu.VMEM((T, D), BF16),
            dma((2,)), dma((6,)), dma, dma, dma, dma((4,)), dma((4,)), dma((4,)), dma, dma,
            pltpu.SemaphoreType.REGULAR,
        ],
        compiler_params=pltpu.CompilerParams(
            collective_id=0, has_side_effects=True, vmem_limit_bytes=40 * 2**20
        ),
    )(
        *(
            pltpu.with_memory_space_constraint(arg, pltpu.HBM)
            for arg in (
                tokens_in,
                dest_slot.reshape(1, T),
                surrogate.reshape(PAIRS, 128),
                gain_cluster.reshape(1, D),
                gain_summary.reshape(1, D),
                w_query, w_key, w_value,
            )
        )
    )
    return jnp.dot(mixture, w_out, preferred_element_type=F32).astype(BF16)


def solution(mesh):
    in_specs = (P(("gx", "gy"), None), P(("gx", "gy")), P(), P(), P(), P(), P(), P(), P())
    out_specs = P(("gx", "gy"), None)
    return jax.shard_map(body, mesh=mesh, in_specs=in_specs, out_specs=out_specs, check_vma=False)
```

```python
import functools
import math

import jax
import jax.numpy as jnp
from jax import lax
from jax.experimental import pallas as pl
from jax.experimental.pallas import tpu as pltpu
from jax.sharding import PartitionSpec as P

MESH = pl.DeviceIdType.MESH
F32, BF16 = jnp.float32, jnp.bfloat16
GX, GY = 8, 16
N = GX * GY
CHIPS = N // 2
T = 128
D = 1024
HEADS, HD = 16, 64
PAIRS = D // 128
FAR_FIRST = (2, 1, 3, 0)
ROWS_FAR_FIRST = [(dy, dc) for dc in (1, 0) for dy in FAR_FIRST]
CAP = 2
ROWS = N * CAP
PAD = 128.0
MARK = 1024.0
EXP2_SCALE = math.log2(math.e) / math.sqrt(HD)


def iota(shape, dim):
    return lax.broadcasted_iota(jnp.int32, shape, dim).astype(F32)


def dot(a, b):
    return jnp.dot(a, b, preferred_element_type=F32)


def dot_nt(a, b):
    return lax.dot_general(a, b, (((1,), (1,)), ((), ())), preferred_element_type=F32)


def dot_tn(a, b):
    return lax.dot_general(a, b, (((0,), (0,)), ((), ())), preferred_element_type=F32)


def attend_pair(q_tile, k_tile, v_tile, low):
    zero = jnp.zeros_like(q_tile)
    q_two = jnp.concatenate([jnp.where(low, q_tile, zero), jnp.where(low, zero, q_tile)], axis=0)
    scores = dot_nt(q_two, k_tile)
    top = jnp.max(scores, axis=1, keepdims=True)
    raised = jnp.exp2((scores - top) * EXP2_SCALE)
    total = 1.0 / jnp.sum(raised, axis=1, keepdims=True)
    raised = raised.astype(BF16)
    both = jnp.concatenate([raised[:T], raised[T:]], axis=1)
    v_two = jnp.concatenate([jnp.where(low, v_tile, zero), jnp.where(low, zero, v_tile)], axis=0)
    return dot(both, v_two) * jnp.where(low, total[:T], total[T:])


def kernel(
    x_hbm, slot_hbm, surr_hbm, gain_c_hbm, gain_s_hbm, wq_hbm, wk_hbm, wv_hbm,
    out_ref,
    x_ref, slot_ref, surr_ref, gain_c_ref, gain_s_ref, wq, wk, wv, stage, rows, send_buf, recv_buf, back_buf, home_buf, sums_buf, att, q_loc,
    x_sem, w_sem, fwd_send, fwd_recv, sum_send, sum_recv, pass_send, pass_recv, back_send, back_recv, row_sem,
):
    gx, gy = lax.axis_index("gx"), lax.axis_index("gy")

    y, core, x, z = gx // 2, lax.rem(gx, 2), gy // 4, lax.rem(gy, 4)

    def far_first(i):
        a, b = i // 4, lax.rem(i, 4)
        tx = lax.rem(x + 2 + a * (a + 1) // 2, 4)
        return tx * 4 + lax.rem(z + 2 + b * (b + 1) // 2, 4)

    def row_at(dy, dc):
        return lax.rem(y + 4 + dy, 4) * 2 + lax.rem(core + dc, 2)

    mine = core * CHIPS + y * GY + gy

    firsts = [
        pltpu.make_async_copy(src, dst, x_sem.at[i])
        for i, (src, dst) in enumerate(((slot_hbm, slot_ref), (x_hbm, x_ref)))
    ]
    loads = [
        pltpu.make_async_copy(src, dst, w_sem.at[i])
        for i, (src, dst) in enumerate(
            (
                (wq_hbm, wq), (wk_hbm, wk), (wv_hbm, wv),
                (surr_hbm, surr_ref), (gain_c_hbm, gain_c_ref), (gain_s_hbm, gain_s_ref),
            )
        )
    ]
    for load in firsts:
        load.start()

    with jax.named_scope("barrier_a"):
        barrier = pltpu.get_barrier_semaphore()
        for i in range(1, GX):
            pl.semaphore_signal(barrier, inc=1, device_id=(lax.rem(gx + i, GX), gy), device_id_type=MESH)
        for i in range(1, GY):
            pl.semaphore_signal(barrier, inc=1, device_id=(gx, lax.rem(gy + i, GY)), device_id_type=MESH)

    with jax.named_scope("pack"):
        for load in firsts:
            load.wait()
        for load in loads:
            load.start()
        owner = slot_ref[...] >> 7
        steps = ((owner >> 5) + (4 - y)) & 3
        other = ((owner >> 4) + core) & 1
        owner_row = (steps * 32 + other * GY + (owner & (GY - 1))).astype(F32)
        sub, lane = iota((T, T), 0), iota((T, T), 1)
        owner_wide = jnp.broadcast_to(owner_row, (T, T))
        owner_col = jnp.sum(jnp.where(sub == lane, owner_wide, 0.0), axis=1, keepdims=True)
        same = (owner_col == owner_wide).astype(F32)
        place_row = owner_row * CAP + jnp.sum(jnp.where(sub < lane, same, 0.0), axis=0, keepdims=True)
        place_col = owner_col * CAP + jnp.sum(jnp.where(lane < sub, same, 0.0), axis=1, keepdims=True)
        pick = (iota((ROWS, T), 0) == place_row).astype(F32)
        filled = jnp.sum(pick, axis=1, keepdims=True) > 0.5
        pick = pick.astype(BF16)
        for j in range(PAIRS):
            part = dot(pick, x_ref[:, j * 128 : (j + 1) * 128])
            stage[pl.ds(j, ROWS, stride=8), :] = jnp.where(filled, part, PAD)
        send_buf[...] = stage[...].astype(BF16).reshape(N, 16, 128)

    with jax.named_scope("barrier_b"):
        pl.semaphore_wait(barrier, GX + GY - 2)
        for i in range(1, GX):
            pl.semaphore_signal(row_sem, inc=1, device_id=(lax.rem(gx + i, GX), gy), device_id_type=MESH)
        pl.semaphore_wait(row_sem, GX - 1)

    def to_all(src, dst, send_sem, recv_sems, sign):
        for dy, dc in ROWS_FAR_FIRST:

            def send(i, carry, dy=dy, dc=dc):
                ty = far_first(i)
                pltpu.make_async_remote_copy(
                    src_ref=src.at[(dy * 2 + dc) * GY + ty],
                    dst_ref=dst.at[(dy * 2 + dc) * GY + gy],
                    send_sem=send_sem,
                    recv_sem=recv_sems.at[dy * 2 + dc],
                    device_id=(row_at(sign * dy, dc), ty),
                    device_id_type=MESH,
                ).start()
                return carry

            lax.fori_loop(0, GY if dy + dc else GY - 1, send, 0)
        dst[pl.ds(gy, 1)] = src[pl.ds(gy, 1)]

    def wait_for(buf, count, sem):
        some = buf.at[pl.ds(0, count)]
        pltpu.make_async_copy(some, some, sem).wait()

    def wait_all(buf, sem):
        wait_for(buf, N - 1, sem)

    def unpack(buf, recv_sems):
        for dy, dc in ROWS_FAR_FIRST:
            g = dy * 2 + dc
            wait_for(buf, GY - 1 if g == 0 else GY, recv_sems.at[g])
            tiles = buf[g * GY : (g + 1) * GY].astype(F32).reshape(GY * 16, 128)
            stage[g * GY * 16 : (g + 1) * GY * 16, :] = tiles
            for j in range(PAIRS):
                part = stage[pl.ds(g * GY * 16 + j, GY * CAP, stride=8), :]
                rows[g * GY * CAP : (g + 1) * GY * CAP, j * 128 : (j + 1) * 128] = part.astype(BF16)

    with jax.named_scope("send_tokens"):
        to_all(send_buf, recv_buf, fwd_send, fwd_recv, 1)

    with jax.named_scope("local_query"):
        loads[0].wait()
        q_loc[...] = dot(x_ref[...], wq[...]).astype(BF16)

    with jax.named_scope("pool_weights"):
        own = lax.broadcasted_iota(jnp.int32, (HEADS, D), 1) // HD == lax.broadcasted_iota(
            jnp.int32, (HEADS, D), 0
        )
        loads[3].wait()
        surr = surr_ref[...].astype(F32)
        surr = jnp.concatenate([surr[j : j + 1] for j in range(PAIRS)], axis=1)
        anchor = jnp.where(own, jnp.broadcast_to(surr, (HEADS, D)), 0.0).astype(BF16)
        loads[1].wait()
        pool_w = dot_nt(anchor, wk[...]).astype(BF16)

    with jax.named_scope("unpack"):
        unpack(recv_buf, fwd_recv)
        real = (rows[:, :128].astype(F32) < 100.0).astype(BF16)
        r_sub, r_lane = iota((ROWS, ROWS), 0), iota((ROWS, ROWS), 1)
        mark = jnp.where(r_sub == r_lane, -MARK, 0.0)
        rank_row = dot_tn(real, (mark + (r_sub < r_lane).astype(F32)).astype(BF16))
        rank_col = dot((mark + (r_lane < r_sub).astype(F32)).astype(BF16), real)
        gather = (rank_row == iota((T, ROWS), 0) - MARK).astype(BF16)
        scatter = (rank_col == iota((ROWS, T), 1) - MARK).astype(BF16)
        members = dot(gather, rows[...]).astype(BF16)

    with jax.named_scope("key_value"):
        logits = dot_nt(pool_w, members)
        raised = jnp.exp2((logits - jnp.max(logits, axis=1, keepdims=True)) * EXP2_SCALE)
        pooled = (raised / jnp.sum(raised, axis=1, keepdims=True)).astype(BF16)
        key = dot(members, wk[...]).astype(BF16)
        loads[2].wait()
        value = dot(members, wv[...]).astype(BF16)

    with jax.named_scope("summary"):
        key_sum = jnp.where(own, dot(pooled, key), 0.0)
        key_sum = key_sum * lax.rsqrt(jnp.sum(key_sum * key_sum, axis=1, keepdims=True) / HD + 1e-6)
        key_sum = jnp.sum(key_sum, axis=0, keepdims=True)
        value_sum = jnp.sum(jnp.where(own, dot(pooled, value), 0.0), axis=0, keepdims=True)
        for j in range(PAIRS):
            stage[j : j + 1, :] = key_sum[:, j * 128 : (j + 1) * 128]
            stage[8 + j : 9 + j, :] = value_sum[:, j * 128 : (j + 1) * 128]
        sums_buf[pl.ds(mine, 1)] = stage[:16, :].astype(BF16)[None]
    with jax.named_scope("send_summary"):
        for dy in FAR_FIRST:

            def send(i, carry, dy=dy):
                pltpu.make_async_remote_copy(
                    src_ref=sums_buf.at[mine],
                    dst_ref=sums_buf.at[mine],
                    send_sem=sum_send,
                    recv_sem=sum_recv.at[dy],
                    device_id=(row_at(dy, 0), far_first(i)),
                    device_id_type=MESH,
                ).start()
                return carry

            lax.fori_loop(0, GY if dy else GY - 1, send, 0)

    low = lax.broadcasted_iota(jnp.int32, (T, 128), 1) < HD

    with jax.named_scope("query"):
        query = dot(members, wq[...]).astype(BF16)
    with jax.named_scope("attend"):
        square = jnp.zeros((T, 128), F32)
        for j in range(PAIRS):
            at = slice(j * 128, (j + 1) * 128)
            got = attend_pair(query[:, at], key[:, at], value[:, at], low)
            square = square + got * got
            att[:, at] = got
        scale = lax.rsqrt(jnp.sum(square, axis=1, keepdims=True) / D + 1e-6)
        loads[4].wait()
        branch = (att[...] * scale * gain_c_ref[...]).astype(BF16)
    with jax.named_scope("pack_back"):
        for j in range(PAIRS):
            stage[pl.ds(j, ROWS, stride=8), :] = dot(scatter, branch[:, j * 128 : (j + 1) * 128])
        back_buf[...] = stage[...].astype(BF16).reshape(N, 16, 128)
    with jax.named_scope("send_back"):
        to_all(back_buf, home_buf, back_send, back_recv, -1)

    with jax.named_scope("pass_summary"):
        passes = []
        for dy in FAR_FIRST:
            wait_for(sums_buf, GY - 1 if dy == 0 else GY, sum_recv.at[dy])
            block = sums_buf.at[pl.ds(core * CHIPS + lax.rem(y + 4 - dy, 4) * GY, GY)]
            passes.append(
                pltpu.make_async_remote_copy(
                    src_ref=block,
                    dst_ref=block,
                    send_sem=pass_send.at[dy],
                    recv_sem=pass_recv.at[dy],
                    device_id=(gx + 1 - 2 * core, gy),
                    device_id_type=MESH,
                )
            )
            passes[-1].start()
        for one in passes:
            one.wait()
    with jax.named_scope("attend_summary"):
        stage[...] = sums_buf[...].astype(F32).reshape(N * 16, 128)
        square = jnp.zeros((T, 128), F32)
        for j in range(PAIRS):
            at = slice(j * 128, (j + 1) * 128)
            got = attend_pair(
                q_loc[:, at],
                stage[pl.ds(j, N, stride=16), :].astype(BF16),
                stage[pl.ds(8 + j, N, stride=16), :].astype(BF16),
                low,
            )
            square = square + got * got
            att[:, at] = got
        scale = lax.rsqrt(jnp.sum(square, axis=1, keepdims=True) / D + 1e-6)
        loads[5].wait()
        att[...] = att[...] * scale * gain_s_ref[...]

    with jax.named_scope("mix_out"):
        unpack(home_buf, back_recv)
        pick_back = (iota((T, ROWS), 1) == place_col).astype(BF16)
        mixture = (dot(pick_back, rows[...]) + att[...]).astype(BF16)
        out_ref[...] = mixture

    with jax.named_scope("drain"):
        wait_all(send_buf, fwd_send)
        wait_for(sums_buf, CHIPS - 1, sum_send)
        wait_all(back_buf, back_send)


def body(
    tokens_in, dest_slot, w_query, w_key, w_value, surrogate, gain_cluster, gain_summary, w_out
):
    vmem, hbm = pl.BlockSpec(memory_space=pltpu.VMEM), pl.BlockSpec(memory_space=pl.ANY)
    tiles = pltpu.VMEM((N, 16, 128), BF16)
    weight = pltpu.VMEM((D, D), BF16)
    dma = pltpu.SemaphoreType.DMA
    mixture = pl.pallas_call(
        kernel,
        out_shape=jax.ShapeDtypeStruct((T, D), BF16),
        in_specs=[hbm] * 8,
        out_specs=vmem,
        scratch_shapes=[
            pltpu.VMEM((T, D), BF16),
            pltpu.VMEM((1, T), jnp.int32),
            pltpu.VMEM((PAIRS, 128), BF16),
            pltpu.VMEM((1, D), F32),
            pltpu.VMEM((1, D), F32),
        ]
        + [weight] * 3
        + [
            pltpu.VMEM((ROWS * 8, 128), F32),
            pltpu.VMEM((ROWS, D), BF16),
            tiles, tiles, tiles, tiles,
            tiles,
            pltpu.VMEM((T, D), F32),
            pltpu.VMEM((T, D), BF16),
            dma((2,)), dma((6,)), dma, dma((GX,)), dma, dma((4,)), dma((4,)), dma((4,)), dma, dma((GX,)),
            pltpu.SemaphoreType.REGULAR,
        ],
        compiler_params=pltpu.CompilerParams(
            collective_id=0, has_side_effects=True, vmem_limit_bytes=40 * 2**20
        ),
    )(
        *(
            pltpu.with_memory_space_constraint(arg, pltpu.HBM)
            for arg in (
                tokens_in,
                dest_slot.reshape(1, T),
                surrogate.reshape(PAIRS, 128),
                gain_cluster.reshape(1, D),
                gain_summary.reshape(1, D),
                w_query, w_key, w_value,
            )
        )
    )
    return jnp.dot(mixture, w_out, preferred_element_type=F32).astype(BF16)


def solution(mesh):
    in_specs = (P(("gx", "gy"), None), P(("gx", "gy")), P(), P(), P(), P(), P(), P(), P())
    out_specs = P(("gx", "gy"), None)
    return jax.shard_map(body, mesh=mesh, in_specs=in_specs, out_specs=out_specs, check_vma=False)
```

```python
import functools
import math

import jax
import jax.numpy as jnp
from jax import lax
from jax.experimental import pallas as pl
from jax.experimental.pallas import tpu as pltpu
from jax.sharding import PartitionSpec as P

MESH = pl.DeviceIdType.MESH
F32, BF16 = jnp.float32, jnp.bfloat16
GX, GY = 8, 16
N = GX * GY
CHIPS = N // 2
T = 128
D = 1024
HEADS, HD = 16, 64
PAIRS = D // 128
FAR_FIRST = (2, 1, 3, 0)
ROWS_FAR_FIRST = [(dy, dc) for dc in (1, 0) for dy in FAR_FIRST]
CAP = 2
ROWS = N * CAP
PAD = 128.0
MARK = 1024.0
EXP2_SCALE = math.log2(math.e) / math.sqrt(HD)


def iota(shape, dim):
    return lax.broadcasted_iota(jnp.int32, shape, dim).astype(F32)


def dot(a, b):
    return jnp.dot(a, b, preferred_element_type=F32)


def dot_nt(a, b):
    return lax.dot_general(a, b, (((1,), (1,)), ((), ())), preferred_element_type=F32)


def dot_tn(a, b):
    return lax.dot_general(a, b, (((0,), (0,)), ((), ())), preferred_element_type=F32)


def attend_pair(q_tile, k_tile, v_tile, low):
    zero = jnp.zeros_like(q_tile)
    q_two = jnp.concatenate([jnp.where(low, q_tile, zero), jnp.where(low, zero, q_tile)], axis=0)
    scores = dot_nt(q_two, k_tile)
    top = jnp.max(scores, axis=1, keepdims=True)
    raised = jnp.exp2((scores - top) * EXP2_SCALE)
    total = 1.0 / jnp.sum(raised, axis=1, keepdims=True)
    raised = raised.astype(BF16)
    both = jnp.concatenate([raised[:T], raised[T:]], axis=1)
    v_two = jnp.concatenate([jnp.where(low, v_tile, zero), jnp.where(low, zero, v_tile)], axis=0)
    return dot(both, v_two) * jnp.where(low, total[:T], total[T:])


def kernel(
    x_hbm, slot_hbm, surr_hbm, gain_c_hbm, gain_s_hbm, wq_hbm, wk_hbm, wv_hbm,
    out_ref,
    x_ref, slot_ref, surr_ref, gain_c_ref, gain_s_ref, wq, wk, wv, stage, rows, send_buf, recv_buf, back_buf, home_buf, sums_buf, att, q_loc,
    x_sem, w_sem, fwd_send, fwd_recv, sum_send, sum_recv, pass_send, pass_recv, back_send, back_recv,
):
    gx, gy = lax.axis_index("gx"), lax.axis_index("gy")

    y, core, x, z = gx // 2, lax.rem(gx, 2), gy // 4, lax.rem(gy, 4)

    xs = [lax.rem(x + d, 4) * 4 for d in range(4)]
    zs = [lax.rem(z + d, 4) for d in range(4)]

    def row_at(dy, dc):
        return lax.rem(y + 4 + dy, 4) * 2 + lax.rem(core + dc, 2)

    mine = core * CHIPS + y * GY + gy

    firsts = [
        pltpu.make_async_copy(src, dst, x_sem.at[i])
        for i, (src, dst) in enumerate(((slot_hbm, slot_ref), (x_hbm, x_ref)))
    ]
    loads = [
        pltpu.make_async_copy(src, dst, w_sem.at[i])
        for i, (src, dst) in enumerate(
            (
                (wq_hbm, wq), (wk_hbm, wk), (wv_hbm, wv),
                (surr_hbm, surr_ref), (gain_c_hbm, gain_c_ref), (gain_s_hbm, gain_s_ref),
            )
        )
    ]
    for load in firsts:
        load.start()

    with jax.named_scope("barrier_signal"):
        barrier = pltpu.get_barrier_semaphore()
        for dy in FAR_FIRST:
            for dx in FAR_FIRST:
                for dz in FAR_FIRST:
                    for dc in (1, 0):
                        if dy or dx or dz or dc:
                            there = (row_at(dy, dc), xs[dx] + zs[dz])
                            pl.semaphore_signal(barrier, inc=1, device_id=there, device_id_type=MESH)

    with jax.named_scope("pack"):
        for load in firsts:
            load.wait()
        for load in loads:
            load.start()
        owner = slot_ref[...] >> 7
        steps = ((owner >> 5) + (4 - y)) & 3
        other = ((owner >> 4) + core) & 1
        owner_row = (steps * 32 + other * GY + (owner & (GY - 1))).astype(F32)
        sub, lane = iota((T, T), 0), iota((T, T), 1)
        owner_wide = jnp.broadcast_to(owner_row, (T, T))
        owner_col = jnp.sum(jnp.where(sub == lane, owner_wide, 0.0), axis=1, keepdims=True)
        same = (owner_col == owner_wide).astype(F32)
        place_row = owner_row * CAP + jnp.sum(jnp.where(sub < lane, same, 0.0), axis=0, keepdims=True)
        place_col = owner_col * CAP + jnp.sum(jnp.where(lane < sub, same, 0.0), axis=1, keepdims=True)
        pick = (iota((ROWS, T), 0) == place_row).astype(F32)
        filled = jnp.sum(pick, axis=1, keepdims=True) > 0.5
        pick = pick.astype(BF16)
        for j in range(PAIRS):
            part = dot(pick, x_ref[:, j * 128 : (j + 1) * 128])
            stage[pl.ds(j, ROWS, stride=8), :] = jnp.where(filled, part, PAD)
        send_buf[...] = stage[...].astype(BF16).reshape(N, 16, 128)

    with jax.named_scope("barrier_wait"):
        pl.semaphore_wait(barrier, N - 1)

    def to_all(src, dst, send_sem, recv_sems, sign):
        for dy, dc in ROWS_FAR_FIRST:
            there = row_at(sign * dy, dc)
            for dx in FAR_FIRST:
                for dz in FAR_FIRST:
                    if dy or dc or dx or dz:
                        ty = xs[dx] + zs[dz]
                        pltpu.make_async_remote_copy(
                            src_ref=src.at[(dy * 2 + dc) * GY + ty],
                            dst_ref=dst.at[(dy * 2 + dc) * GY + gy],
                            send_sem=send_sem,
                            recv_sem=recv_sems.at[dy * 2 + dc],
                            device_id=(there, ty),
                            device_id_type=MESH,
                        ).start()
        dst[pl.ds(gy, 1)] = src[pl.ds(gy, 1)]

    def wait_for(buf, count, sem):
        some = buf.at[pl.ds(0, count)]
        pltpu.make_async_copy(some, some, sem).wait()

    def wait_all(buf, sem):
        wait_for(buf, N - 1, sem)

    def unpack(buf, recv_sems):
        for dy, dc in ROWS_FAR_FIRST:
            g = dy * 2 + dc
            wait_for(buf, GY - 1 if g == 0 else GY, recv_sems.at[g])
            tiles = buf[g * GY : (g + 1) * GY].astype(F32).reshape(GY * 16, 128)
            stage[g * GY * 16 : (g + 1) * GY * 16, :] = tiles
            for j in range(PAIRS):
                part = stage[pl.ds(g * GY * 16 + j, GY * CAP, stride=8), :]
                rows[g * GY * CAP : (g + 1) * GY * CAP, j * 128 : (j + 1) * 128] = part.astype(BF16)

    with jax.named_scope("send_tokens"):
        to_all(send_buf, recv_buf, fwd_send, fwd_recv, 1)

    with jax.named_scope("local_query"):
        loads[0].wait()
        q_loc[...] = dot(x_ref[...], wq[...]).astype(BF16)

    with jax.named_scope("pool_weights"):
        own = lax.broadcasted_iota(jnp.int32, (HEADS, D), 1) // HD == lax.broadcasted_iota(
            jnp.int32, (HEADS, D), 0
        )
        loads[3].wait()
        surr = surr_ref[...].astype(F32)
        surr = jnp.concatenate([surr[j : j + 1] for j in range(PAIRS)], axis=1)
        anchor = jnp.where(own, jnp.broadcast_to(surr, (HEADS, D)), 0.0).astype(BF16)
        for load in loads[1:3] + loads[4:]:
            load.wait()

    with jax.named_scope("unpack"):
        unpack(recv_buf, fwd_recv)
        real = (rows[:, :128].astype(F32) < 100.0).astype(BF16)
        r_sub, r_lane = iota((ROWS, ROWS), 0), iota((ROWS, ROWS), 1)
        mark = jnp.where(r_sub == r_lane, -MARK, 0.0)
        rank_row = dot_tn(real, (mark + (r_sub < r_lane).astype(F32)).astype(BF16))
        rank_col = dot((mark + (r_lane < r_sub).astype(F32)).astype(BF16), real)
        gather = (rank_row == iota((T, ROWS), 0) - MARK).astype(BF16)
        scatter = (rank_col == iota((ROWS, T), 1) - MARK).astype(BF16)
        members = dot(gather, rows[...]).astype(BF16)

    with jax.named_scope("key_value"):
        key = dot(members, wk[...]).astype(BF16)
        logits = dot_nt(anchor, key)
        raised = jnp.exp2((logits - jnp.max(logits, axis=1, keepdims=True)) * EXP2_SCALE)
        pooled = (raised / jnp.sum(raised, axis=1, keepdims=True)).astype(BF16)
        value = dot(members, wv[...]).astype(BF16)

    with jax.named_scope("summary"):
        key_sum = jnp.where(own, dot(pooled, key), 0.0)
        key_sum = key_sum * lax.rsqrt(jnp.sum(key_sum * key_sum, axis=1, keepdims=True) / HD + 1e-6)
        key_sum = jnp.sum(key_sum, axis=0, keepdims=True)
        value_sum = jnp.sum(jnp.where(own, dot(pooled, value), 0.0), axis=0, keepdims=True)
        for j in range(PAIRS):
            stage[j : j + 1, :] = key_sum[:, j * 128 : (j + 1) * 128]
            stage[8 + j : 9 + j, :] = value_sum[:, j * 128 : (j + 1) * 128]
        sums_buf[pl.ds(mine, 1)] = stage[:16, :].astype(BF16)[None]
    with jax.named_scope("send_summary"):
        for dy in FAR_FIRST:
            there = row_at(dy, 0)
            for dx in FAR_FIRST:
                for dz in FAR_FIRST:
                    if dy or dx or dz:
                        pltpu.make_async_remote_copy(
                            src_ref=sums_buf.at[mine],
                            dst_ref=sums_buf.at[mine],
                            send_sem=sum_send,
                            recv_sem=sum_recv.at[dy],
                            device_id=(there, xs[dx] + zs[dz]),
                            device_id_type=MESH,
                        ).start()

    low = lax.broadcasted_iota(jnp.int32, (T, 128), 1) < HD

    with jax.named_scope("query"):
        query = dot(members, wq[...]).astype(BF16)
    with jax.named_scope("attend"):
        square = jnp.zeros((T, 128), F32)
        for j in range(PAIRS):
            at = slice(j * 128, (j + 1) * 128)
            got = attend_pair(query[:, at], key[:, at], value[:, at], low)
            square = square + got * got
            att[:, at] = got
        scale = lax.rsqrt(jnp.sum(square, axis=1, keepdims=True) / D + 1e-6)
        branch = (att[...] * scale * gain_c_ref[...]).astype(BF16)
    with jax.named_scope("pack_back"):
        for j in range(PAIRS):
            stage[pl.ds(j, ROWS, stride=8), :] = dot(scatter, branch[:, j * 128 : (j + 1) * 128])
        back_buf[...] = stage[...].astype(BF16).reshape(N, 16, 128)
    with jax.named_scope("send_back"):
        to_all(back_buf, home_buf, back_send, back_recv, -1)

    with jax.named_scope("pass_summary"):
        passes = []
        for dy in FAR_FIRST:
            wait_for(sums_buf, GY - 1 if dy == 0 else GY, sum_recv.at[dy])
            block = sums_buf.at[pl.ds(core * CHIPS + lax.rem(y + 4 - dy, 4) * GY, GY)]
            passes.append(
                pltpu.make_async_remote_copy(
                    src_ref=block,
                    dst_ref=block,
                    send_sem=pass_send.at[dy],
                    recv_sem=pass_recv.at[dy],
                    device_id=(gx + 1 - 2 * core, gy),
                    device_id_type=MESH,
                )
            )
            passes[-1].start()
        for one in passes:
            one.wait()
    with jax.named_scope("attend_summary"):
        stage[...] = sums_buf[...].astype(F32).reshape(N * 16, 128)
        square = jnp.zeros((T, 128), F32)
        for j in range(PAIRS):
            at = slice(j * 128, (j + 1) * 128)
            got = attend_pair(
                q_loc[:, at],
                stage[pl.ds(j, N, stride=16), :].astype(BF16),
                stage[pl.ds(8 + j, N, stride=16), :].astype(BF16),
                low,
            )
            square = square + got * got
            att[:, at] = got
        scale = lax.rsqrt(jnp.sum(square, axis=1, keepdims=True) / D + 1e-6)
        att[...] = att[...] * scale * gain_s_ref[...]

    with jax.named_scope("mix_out"):
        unpack(home_buf, back_recv)
        pick_back = (iota((T, ROWS), 1) == place_col).astype(BF16)
        mixture = (dot(pick_back, rows[...]) + att[...]).astype(BF16)
        out_ref[...] = mixture

    with jax.named_scope("drain"):
        wait_all(send_buf, fwd_send)
        wait_for(sums_buf, CHIPS - 1, sum_send)
        wait_all(back_buf, back_send)


def body(
    tokens_in, dest_slot, w_query, w_key, w_value, surrogate, gain_cluster, gain_summary, w_out
):
    vmem, hbm = pl.BlockSpec(memory_space=pltpu.VMEM), pl.BlockSpec(memory_space=pl.ANY)
    tiles = pltpu.VMEM((N, 16, 128), BF16)
    weight = pltpu.VMEM((D, D), BF16)
    dma = pltpu.SemaphoreType.DMA
    mixture = pl.pallas_call(
        kernel,
        out_shape=jax.ShapeDtypeStruct((T, D), BF16),
        in_specs=[hbm] * 8,
        out_specs=vmem,
        scratch_shapes=[
            pltpu.VMEM((T, D), BF16),
            pltpu.VMEM((1, T), jnp.int32),
            pltpu.VMEM((PAIRS, 128), BF16),
            pltpu.VMEM((1, D), F32),
            pltpu.VMEM((1, D), F32),
        ]
        + [weight] * 3
        + [
            pltpu.VMEM((ROWS * 8, 128), F32),
            pltpu.VMEM((ROWS, D), BF16),
            tiles, tiles, tiles, tiles,
            tiles,
            pltpu.VMEM((T, D), F32),
            pltpu.VMEM((T, D), BF16),
            dma((2,)), dma((6,)), dma, dma((GX,)), dma, dma((4,)), dma((4,)), dma((4,)), dma, dma((GX,)),
        ],
        compiler_params=pltpu.CompilerParams(
            collective_id=0, has_side_effects=True, vmem_limit_bytes=40 * 2**20
        ),
    )(
        *(
            pltpu.with_memory_space_constraint(arg, pltpu.HBM)
            for arg in (
                tokens_in,
                dest_slot.reshape(1, T),
                surrogate.reshape(PAIRS, 128),
                gain_cluster.reshape(1, D),
                gain_summary.reshape(1, D),
                w_query, w_key, w_value,
            )
        )
    )
    return jnp.dot(mixture, w_out, preferred_element_type=F32).astype(BF16)


def solution(mesh):
    in_specs = (P(("gx", "gy"), None), P(("gx", "gy")), P(), P(), P(), P(), P(), P(), P())
    out_specs = P(("gx", "gy"), None)
    return jax.shard_map(body, mesh=mesh, in_specs=in_specs, out_specs=out_specs, check_vma=False)
```

```python
import functools
import math

import jax
import jax.numpy as jnp
from jax import lax
from jax.experimental import pallas as pl
from jax.experimental.pallas import tpu as pltpu
from jax.sharding import PartitionSpec as P

MESH = pl.DeviceIdType.MESH
F32, BF16 = jnp.float32, jnp.bfloat16
GX, GY = 8, 16
N = GX * GY
CHIPS = N // 2
T = 128
D = 1024
HEADS, HD = 16, 64
PAIRS = D // 128
FAR_FIRST = (2, 1, 3, 0)
ROWS_FAR_FIRST = [(dy, dc) for dc in (1, 0) for dy in FAR_FIRST]
CAP = 2
ROWS = N * CAP
PAD = 128.0
MARK = 1024.0
EXP2_SCALE = math.log2(math.e) / math.sqrt(HD)


def iota(shape, dim):
    return lax.broadcasted_iota(jnp.int32, shape, dim).astype(F32)


def dot(a, b):
    return jnp.dot(a, b, preferred_element_type=F32)


def dot_nt(a, b):
    return lax.dot_general(a, b, (((1,), (1,)), ((), ())), preferred_element_type=F32)


def dot_tn(a, b):
    return lax.dot_general(a, b, (((0,), (0,)), ((), ())), preferred_element_type=F32)


def attend_pair(q_tile, k_tile, v_tile, low):
    zero = jnp.zeros_like(q_tile)
    q_two = jnp.concatenate([jnp.where(low, q_tile, zero), jnp.where(low, zero, q_tile)], axis=0)
    scores = dot_nt(q_two, k_tile)
    top = jnp.max(scores, axis=1, keepdims=True)
    raised = jnp.exp2((scores - top) * EXP2_SCALE)
    total = 1.0 / jnp.sum(raised, axis=1, keepdims=True)
    raised = raised.astype(BF16)
    both = jnp.concatenate([raised[:T], raised[T:]], axis=1)
    v_two = jnp.concatenate([jnp.where(low, v_tile, zero), jnp.where(low, zero, v_tile)], axis=0)
    return dot(both, v_two) * jnp.where(low, total[:T], total[T:])


def kernel(
    x_hbm, slot_hbm, surr_hbm, gain_c_hbm, gain_s_hbm, wq_hbm, wk_hbm, wv_hbm, wo_hbm,
    out_ref,
    x_ref, slot_ref, surr_ref, gain_c_ref, gain_s_ref, wq, wk, wv, wo, stage, rows, send_buf, recv_buf, back_buf, home_buf, sums_buf, att, q_loc,
    x_sem, w_sem, fwd_send, fwd_recv, sum_send, sum_recv, pass_send, pass_recv, back_send, back_recv,
):
    gx, gy = lax.axis_index("gx"), lax.axis_index("gy")

    y, core, x, z = gx // 2, lax.rem(gx, 2), gy // 4, lax.rem(gy, 4)

    xs = [lax.rem(x + d, 4) * 4 for d in range(4)]
    zs = [lax.rem(z + d, 4) for d in range(4)]

    def row_at(dy, dc):
        return lax.rem(y + 4 + dy, 4) * 2 + lax.rem(core + dc, 2)

    mine = core * CHIPS + y * GY + gy

    firsts = [
        pltpu.make_async_copy(src, dst, x_sem.at[i])
        for i, (src, dst) in enumerate(((slot_hbm, slot_ref), (x_hbm, x_ref)))
    ]
    loads = [
        pltpu.make_async_copy(src, dst, w_sem.at[i])
        for i, (src, dst) in enumerate(
            (
                (wq_hbm, wq), (wk_hbm, wk), (wv_hbm, wv),
                (surr_hbm, surr_ref), (gain_c_hbm, gain_c_ref), (gain_s_hbm, gain_s_ref), (wo_hbm, wo),
            )
        )
    ]
    for load in firsts:
        load.start()

    with jax.named_scope("barrier_signal"):
        barrier = pltpu.get_barrier_semaphore()
        for dy in FAR_FIRST:
            for dx in FAR_FIRST:
                for dz in FAR_FIRST:
                    for dc in (1, 0):
                        if dy or dx or dz or dc:
                            there = (row_at(dy, dc), xs[dx] + zs[dz])
                            pl.semaphore_signal(barrier, inc=1, device_id=there, device_id_type=MESH)

    with jax.named_scope("pack"):
        for load in firsts:
            load.wait()
        for load in loads:
            load.start()
        owner = slot_ref[...] >> 7
        steps = ((owner >> 5) + (4 - y)) & 3
        other = ((owner >> 4) + core) & 1
        owner_row = (steps * 32 + other * GY + (owner & (GY - 1))).astype(F32)
        sub, lane = iota((T, T), 0), iota((T, T), 1)
        owner_wide = jnp.broadcast_to(owner_row, (T, T))
        owner_col = jnp.sum(jnp.where(sub == lane, owner_wide, 0.0), axis=1, keepdims=True)
        same = (owner_col == owner_wide).astype(F32)
        place_row = owner_row * CAP + jnp.sum(jnp.where(sub < lane, same, 0.0), axis=0, keepdims=True)
        place_col = owner_col * CAP + jnp.sum(jnp.where(lane < sub, same, 0.0), axis=1, keepdims=True)
        pick = (iota((ROWS, T), 0) == place_row).astype(F32)
        filled = jnp.sum(pick, axis=1, keepdims=True) > 0.5
        pick = pick.astype(BF16)
        for j in range(PAIRS):
            part = dot(pick, x_ref[:, j * 128 : (j + 1) * 128])
            stage[pl.ds(j, ROWS, stride=8), :] = jnp.where(filled, part, PAD)
        send_buf[...] = stage[...].astype(BF16).reshape(N, 16, 128)

    with jax.named_scope("barrier_wait"):
        pl.semaphore_wait(barrier, N - 1)

    def to_all(src, dst, send_sem, recv_sems, sign):
        for dy, dc in ROWS_FAR_FIRST:
            there = row_at(sign * dy, dc)
            for dx in FAR_FIRST:
                for dz in FAR_FIRST:
                    if dy or dc or dx or dz:
                        ty = xs[dx] + zs[dz]
                        pltpu.make_async_remote_copy(
                            src_ref=src.at[(dy * 2 + dc) * GY + ty],
                            dst_ref=dst.at[(dy * 2 + dc) * GY + gy],
                            send_sem=send_sem,
                            recv_sem=recv_sems.at[dy * 2 + dc],
                            device_id=(there, ty),
                            device_id_type=MESH,
                        ).start()
        dst[pl.ds(gy, 1)] = src[pl.ds(gy, 1)]

    def wait_for(buf, count, sem):
        some = buf.at[pl.ds(0, count)]
        pltpu.make_async_copy(some, some, sem).wait()

    def wait_all(buf, sem):
        wait_for(buf, N - 1, sem)

    def unpack(buf, recv_sems):
        for dy, dc in ROWS_FAR_FIRST:
            g = dy * 2 + dc
            wait_for(buf, GY - 1 if g == 0 else GY, recv_sems.at[g])
            tiles = buf[g * GY : (g + 1) * GY].astype(F32).reshape(GY * 16, 128)
            stage[g * GY * 16 : (g + 1) * GY * 16, :] = tiles
            for j in range(PAIRS):
                part = stage[pl.ds(g * GY * 16 + j, GY * CAP, stride=8), :]
                rows[g * GY * CAP : (g + 1) * GY * CAP, j * 128 : (j + 1) * 128] = part.astype(BF16)

    with jax.named_scope("send_tokens"):
        to_all(send_buf, recv_buf, fwd_send, fwd_recv, 1)

    with jax.named_scope("local_query"):
        loads[0].wait()
        q_loc[...] = dot(x_ref[...], wq[...]).astype(BF16)

    with jax.named_scope("pool_weights"):
        own = lax.broadcasted_iota(jnp.int32, (HEADS, D), 1) // HD == lax.broadcasted_iota(
            jnp.int32, (HEADS, D), 0
        )
        loads[3].wait()
        surr = surr_ref[...].astype(F32)
        surr = jnp.concatenate([surr[j : j + 1] for j in range(PAIRS)], axis=1)
        anchor = jnp.where(own, jnp.broadcast_to(surr, (HEADS, D)), 0.0).astype(BF16)
        for load in loads[1:3] + loads[4:]:
            load.wait()

    with jax.named_scope("unpack"):
        unpack(recv_buf, fwd_recv)
        real = (rows[:, :128].astype(F32) < 100.0).astype(BF16)
        r_sub, r_lane = iota((ROWS, ROWS), 0), iota((ROWS, ROWS), 1)
        mark = jnp.where(r_sub == r_lane, -MARK, 0.0)
        rank_row = dot_tn(real, (mark + (r_sub < r_lane).astype(F32)).astype(BF16))
        rank_col = dot((mark + (r_lane < r_sub).astype(F32)).astype(BF16), real)
        gather = (rank_row == iota((T, ROWS), 0) - MARK).astype(BF16)
        scatter = (rank_col == iota((ROWS, T), 1) - MARK).astype(BF16)
        members = dot(gather, rows[...]).astype(BF16)

    with jax.named_scope("key_value"):
        key = dot(members, wk[...]).astype(BF16)
        logits = dot_nt(anchor, key)
        raised = jnp.exp2((logits - jnp.max(logits, axis=1, keepdims=True)) * EXP2_SCALE)
        pooled = (raised / jnp.sum(raised, axis=1, keepdims=True)).astype(BF16)
        value = dot(members, wv[...]).astype(BF16)

    with jax.named_scope("summary"):
        key_sum = jnp.where(own, dot(pooled, key), 0.0)
        key_sum = key_sum * lax.rsqrt(jnp.sum(key_sum * key_sum, axis=1, keepdims=True) / HD + 1e-6)
        key_sum = jnp.sum(key_sum, axis=0, keepdims=True)
        value_sum = jnp.sum(jnp.where(own, dot(pooled, value), 0.0), axis=0, keepdims=True)
        for j in range(PAIRS):
            stage[j : j + 1, :] = key_sum[:, j * 128 : (j + 1) * 128]
            stage[8 + j : 9 + j, :] = value_sum[:, j * 128 : (j + 1) * 128]
        sums_buf[pl.ds(mine, 1)] = stage[:16, :].astype(BF16)[None]
    with jax.named_scope("send_summary"):
        for dy in FAR_FIRST:
            there = row_at(dy, 0)
            for dx in FAR_FIRST:
                for dz in FAR_FIRST:
                    if dy or dx or dz:
                        pltpu.make_async_remote_copy(
                            src_ref=sums_buf.at[mine],
                            dst_ref=sums_buf.at[mine],
                            send_sem=sum_send,
                            recv_sem=sum_recv.at[dy],
                            device_id=(there, xs[dx] + zs[dz]),
                            device_id_type=MESH,
                        ).start()

    low = lax.broadcasted_iota(jnp.int32, (T, 128), 1) < HD

    with jax.named_scope("query"):
        query = dot(members, wq[...]).astype(BF16)
    with jax.named_scope("attend"):
        square = jnp.zeros((T, 128), F32)
        for j in range(PAIRS):
            at = slice(j * 128, (j + 1) * 128)
            got = attend_pair(query[:, at], key[:, at], value[:, at], low)
            square = square + got * got
            att[:, at] = got
        scale = lax.rsqrt(jnp.sum(square, axis=1, keepdims=True) / D + 1e-6)
        branch = (att[...] * scale * gain_c_ref[...]).astype(BF16)
        branch = dot(branch, wo[...]).astype(BF16)
    with jax.named_scope("pack_back"):
        for j in range(PAIRS):
            stage[pl.ds(j, ROWS, stride=8), :] = dot(scatter, branch[:, j * 128 : (j + 1) * 128])
        back_buf[...] = stage[...].astype(BF16).reshape(N, 16, 128)
    with jax.named_scope("send_back"):
        to_all(back_buf, home_buf, back_send, back_recv, -1)

    with jax.named_scope("pass_summary"):
        passes = []
        for dy in FAR_FIRST:
            wait_for(sums_buf, GY - 1 if dy == 0 else GY, sum_recv.at[dy])
            block = sums_buf.at[pl.ds(core * CHIPS + lax.rem(y + 4 - dy, 4) * GY, GY)]
            passes.append(
                pltpu.make_async_remote_copy(
                    src_ref=block,
                    dst_ref=block,
                    send_sem=pass_send.at[dy],
                    recv_sem=pass_recv.at[dy],
                    device_id=(gx + 1 - 2 * core, gy),
                    device_id_type=MESH,
                )
            )
            passes[-1].start()
        for one in passes:
            one.wait()
    with jax.named_scope("attend_summary"):
        stage[...] = sums_buf[...].astype(F32).reshape(N * 16, 128)
        square = jnp.zeros((T, 128), F32)
        for j in range(PAIRS):
            at = slice(j * 128, (j + 1) * 128)
            got = attend_pair(
                q_loc[:, at],
                stage[pl.ds(j, N, stride=16), :].astype(BF16),
                stage[pl.ds(8 + j, N, stride=16), :].astype(BF16),
                low,
            )
            square = square + got * got
            att[:, at] = got
        scale = lax.rsqrt(jnp.sum(square, axis=1, keepdims=True) / D + 1e-6)
        summary = (att[...] * scale * gain_s_ref[...]).astype(BF16)
        att[...] = dot(summary, wo[...])

    with jax.named_scope("mix_out"):
        unpack(home_buf, back_recv)
        pick_back = (iota((T, ROWS), 1) == place_col).astype(BF16)
        mixture = (dot(pick_back, rows[...]) + att[...]).astype(BF16)
        out_ref[...] = mixture

    with jax.named_scope("drain"):
        wait_all(send_buf, fwd_send)
        wait_for(sums_buf, CHIPS - 1, sum_send)
        wait_all(back_buf, back_send)


def body(
    tokens_in, dest_slot, w_query, w_key, w_value, surrogate, gain_cluster, gain_summary, w_out
):
    vmem, hbm = pl.BlockSpec(memory_space=pltpu.VMEM), pl.BlockSpec(memory_space=pl.ANY)
    tiles = pltpu.VMEM((N, 16, 128), BF16)
    weight = pltpu.VMEM((D, D), BF16)
    dma = pltpu.SemaphoreType.DMA
    layer_out = pl.pallas_call(
        kernel,
        out_shape=jax.ShapeDtypeStruct((T, D), BF16),
        in_specs=[hbm] * 9,
        out_specs=vmem,
        scratch_shapes=[
            pltpu.VMEM((T, D), BF16),
            pltpu.VMEM((1, T), jnp.int32),
            pltpu.VMEM((PAIRS, 128), BF16),
            pltpu.VMEM((1, D), F32),
            pltpu.VMEM((1, D), F32),
        ]
        + [weight] * 4
        + [
            pltpu.VMEM((ROWS * 8, 128), F32),
            pltpu.VMEM((ROWS, D), BF16),
            tiles, tiles, tiles, tiles,
            tiles,
            pltpu.VMEM((T, D), F32),
            pltpu.VMEM((T, D), BF16),
            dma((2,)), dma((7,)), dma, dma((GX,)), dma, dma((4,)), dma((4,)), dma((4,)), dma, dma((GX,)),
        ],
        compiler_params=pltpu.CompilerParams(
            collective_id=0, has_side_effects=True, vmem_limit_bytes=40 * 2**20
        ),
    )(
        *(
            pltpu.with_memory_space_constraint(arg, pltpu.HBM)
            for arg in (
                tokens_in,
                dest_slot.reshape(1, T),
                surrogate.reshape(PAIRS, 128),
                gain_cluster.reshape(1, D),
                gain_summary.reshape(1, D),
                w_query, w_key, w_value, w_out,
            )
        )
    )
    return layer_out


def solution(mesh):
    in_specs = (P(("gx", "gy"), None), P(("gx", "gy")), P(), P(), P(), P(), P(), P(), P())
    out_specs = P(("gx", "gy"), None)
    return jax.shard_map(body, mesh=mesh, in_specs=in_specs, out_specs=out_specs, check_vma=False)
```

```python
import functools
import math

import jax
import jax.numpy as jnp
from jax import lax
from jax.experimental import pallas as pl
from jax.experimental.pallas import tpu as pltpu
from jax.sharding import PartitionSpec as P

MESH = pl.DeviceIdType.MESH
F32, BF16 = jnp.float32, jnp.bfloat16
GX, GY = 8, 16
N = GX * GY
CHIPS = N // 2
T = 128
D = 1024
HEADS, HD = 16, 64
PAIRS = D // 128
FAR_FIRST = (2, 1, 3, 0)
ROWS_FAR_FIRST = [(dy, dc) for dc in (1, 0) for dy in FAR_FIRST]
CAP = 2
ROWS = N * CAP
PAD = 128.0
MARK = 1024.0
EXP2_SCALE = math.log2(math.e) / math.sqrt(HD)


def iota(shape, dim):
    return lax.broadcasted_iota(jnp.int32, shape, dim).astype(F32)


def dot(a, b):
    return jnp.dot(a, b, preferred_element_type=F32)


def dot_nt(a, b):
    return lax.dot_general(a, b, (((1,), (1,)), ((), ())), preferred_element_type=F32)


def dot_tn(a, b):
    return lax.dot_general(a, b, (((0,), (0,)), ((), ())), preferred_element_type=F32)


def attend_pair(q_tile, k_tile, v_tile, low):
    zero = jnp.zeros_like(q_tile)
    q_two = jnp.concatenate([jnp.where(low, q_tile, zero), jnp.where(low, zero, q_tile)], axis=0)
    scores = dot_nt(q_two, k_tile)
    top = jnp.max(scores, axis=1, keepdims=True)
    raised = jnp.exp2((scores - top) * EXP2_SCALE)
    total = 1.0 / jnp.sum(raised, axis=1, keepdims=True)
    raised = raised.astype(BF16)
    both = jnp.concatenate([raised[:T], raised[T:]], axis=1)
    v_two = jnp.concatenate([jnp.where(low, v_tile, zero), jnp.where(low, zero, v_tile)], axis=0)
    return dot(both, v_two) * jnp.where(low, total[:T], total[T:])


def kernel(
    x_hbm, slot_hbm, surr_hbm, gain_c_hbm, gain_s_hbm, wq_hbm, wk_hbm, wv_hbm, wo_hbm,
    out_ref,
    x_ref, slot_ref, surr_ref, gain_c_ref, gain_s_ref, wq, wk, wv, wo, stage, rows, send_buf, recv_buf, back_buf, home_buf, sums_buf, att, q_loc,
    x_sem, w_sem, fwd_send, fwd_recv, sum_send, sum_recv, pass_send, pass_recv, back_send, back_recv,
):
    gx, gy = lax.axis_index("gx"), lax.axis_index("gy")

    y, core, x, z = gx // 2, lax.rem(gx, 2), gy // 4, lax.rem(gy, 4)

    xs = [lax.rem(x + d, 4) * 4 for d in range(4)]
    zs = [lax.rem(z + d, 4) for d in range(4)]

    def row_at(dy, dc):
        return lax.rem(y + 4 + dy, 4) * 2 + lax.rem(core + dc, 2)

    mine = core * CHIPS + y * GY + gy

    firsts = [
        pltpu.make_async_copy(src, dst, x_sem.at[i])
        for i, (src, dst) in enumerate(((slot_hbm, slot_ref), (x_hbm, x_ref)))
    ]
    loads = [
        pltpu.make_async_copy(src, dst, w_sem.at[i])
        for i, (src, dst) in enumerate(
            (
                (wq_hbm, wq), (wk_hbm, wk), (wv_hbm, wv),
                (surr_hbm, surr_ref), (gain_c_hbm, gain_c_ref), (gain_s_hbm, gain_s_ref), (wo_hbm, wo),
            )
        )
    ]
    for load in firsts:
        load.start()

    with jax.named_scope("barrier_signal"):
        barrier = pltpu.get_barrier_semaphore()
        everyone = [
            (dy, dx, dz, dc) for dy in FAR_FIRST for dx in FAR_FIRST for dz in FAR_FIRST for dc in (1, 0)
        ]
        for dy, dx, dz, dc in sorted(everyone, key=lambda d: -sum(min(v, 4 - v) for v in d[:3])):
            if dy or dx or dz or dc:
                there = (row_at(dy, dc), xs[dx] + zs[dz])
                pl.semaphore_signal(barrier, inc=1, device_id=there, device_id_type=MESH)

    with jax.named_scope("pack"):
        for load in firsts:
            load.wait()
        for load in loads:
            load.start()
        owner = slot_ref[...] >> 7
        steps = ((owner >> 5) + (4 - y)) & 3
        other = ((owner >> 4) + core) & 1
        owner_row = (steps * 32 + other * GY + (owner & (GY - 1))).astype(F32)
        sub, lane = iota((T, T), 0), iota((T, T), 1)
        owner_wide = jnp.broadcast_to(owner_row, (T, T))
        owner_col = jnp.sum(jnp.where(sub == lane, owner_wide, 0.0), axis=1, keepdims=True)
        same = (owner_col == owner_wide).astype(F32)
        place_row = owner_row * CAP + jnp.sum(jnp.where(sub < lane, same, 0.0), axis=0, keepdims=True)
        place_col = owner_col * CAP + jnp.sum(jnp.where(lane < sub, same, 0.0), axis=1, keepdims=True)
        pick = (iota((ROWS, T), 0) == place_row).astype(F32)
        filled = jnp.sum(pick, axis=1, keepdims=True) > 0.5
        pick = pick.astype(BF16)
        for j in range(PAIRS):
            part = dot(pick, x_ref[:, j * 128 : (j + 1) * 128])
            stage[pl.ds(j, ROWS, stride=8), :] = jnp.where(filled, part, PAD)
        send_buf[...] = stage[...].astype(BF16).reshape(N, 16, 128)

    with jax.named_scope("barrier_wait"):
        pl.semaphore_wait(barrier, N - 1)

    def to_all(src, dst, send_sem, recv_sems, sign):
        for dy, dc in ROWS_FAR_FIRST:
            there = row_at(sign * dy, dc)
            for dx in FAR_FIRST:
                for dz in FAR_FIRST:
                    if dy or dc or dx or dz:
                        ty = xs[dx] + zs[dz]
                        pltpu.make_async_remote_copy(
                            src_ref=src.at[(dy * 2 + dc) * GY + ty],
                            dst_ref=dst.at[(dy * 2 + dc) * GY + gy],
                            send_sem=send_sem,
                            recv_sem=recv_sems.at[dy * 2 + dc],
                            device_id=(there, ty),
                            device_id_type=MESH,
                        ).start()
        dst[pl.ds(gy, 1)] = src[pl.ds(gy, 1)]

    def wait_for(buf, count, sem):
        some = buf.at[pl.ds(0, count)]
        pltpu.make_async_copy(some, some, sem).wait()

    def wait_all(buf, sem):
        wait_for(buf, N - 1, sem)

    def unpack(buf, recv_sems):
        for dy, dc in ROWS_FAR_FIRST:
            g = dy * 2 + dc
            wait_for(buf, GY - 1 if g == 0 else GY, recv_sems.at[g])
            tiles = buf[g * GY : (g + 1) * GY].astype(F32).reshape(GY * 16, 128)
            stage[g * GY * 16 : (g + 1) * GY * 16, :] = tiles
            for j in range(PAIRS):
                part = stage[pl.ds(g * GY * 16 + j, GY * CAP, stride=8), :]
                rows[g * GY * CAP : (g + 1) * GY * CAP, j * 128 : (j + 1) * 128] = part.astype(BF16)

    with jax.named_scope("send_tokens"):
        to_all(send_buf, recv_buf, fwd_send, fwd_recv, 1)

    with jax.named_scope("local_query"):
        loads[0].wait()
        q_loc[...] = dot(x_ref[...], wq[...]).astype(BF16)

    with jax.named_scope("pool_weights"):
        own = lax.broadcasted_iota(jnp.int32, (HEADS, D), 1) // HD == lax.broadcasted_iota(
            jnp.int32, (HEADS, D), 0
        )
        loads[3].wait()
        surr = surr_ref[...].astype(F32)
        surr = jnp.concatenate([surr[j : j + 1] for j in range(PAIRS)], axis=1)
        anchor = jnp.where(own, jnp.broadcast_to(surr, (HEADS, D)), 0.0).astype(BF16)
        for load in loads[1:3] + loads[4:]:
            load.wait()

    with jax.named_scope("unpack"):
        unpack(recv_buf, fwd_recv)
        real = (rows[:, :128].astype(F32) < 100.0).astype(BF16)
        r_sub, r_lane = iota((ROWS, ROWS), 0), iota((ROWS, ROWS), 1)
        mark = jnp.where(r_sub == r_lane, -MARK, 0.0)
        rank_row = dot_tn(real, (mark + (r_sub < r_lane).astype(F32)).astype(BF16))
        rank_col = dot((mark + (r_lane < r_sub).astype(F32)).astype(BF16), real)
        gather = (rank_row == iota((T, ROWS), 0) - MARK).astype(BF16)
        scatter = (rank_col == iota((ROWS, T), 1) - MARK).astype(BF16)
        members = dot(gather, rows[...]).astype(BF16)

    with jax.named_scope("key_value"):
        key = dot(members, wk[...]).astype(BF16)
        logits = dot_nt(anchor, key)
        raised = jnp.exp2((logits - jnp.max(logits, axis=1, keepdims=True)) * EXP2_SCALE)
        pooled = (raised / jnp.sum(raised, axis=1, keepdims=True)).astype(BF16)
        value = dot(members, wv[...]).astype(BF16)

    with jax.named_scope("summary"):
        key_sum = jnp.where(own, dot(pooled, key), 0.0)
        key_sum = key_sum * lax.rsqrt(jnp.sum(key_sum * key_sum, axis=1, keepdims=True) / HD + 1e-6)
        key_sum = jnp.sum(key_sum, axis=0, keepdims=True)
        value_sum = jnp.sum(jnp.where(own, dot(pooled, value), 0.0), axis=0, keepdims=True)
        for j in range(PAIRS):
            stage[j : j + 1, :] = key_sum[:, j * 128 : (j + 1) * 128]
            stage[8 + j : 9 + j, :] = value_sum[:, j * 128 : (j + 1) * 128]
        sums_buf[pl.ds(mine, 1)] = stage[:16, :].astype(BF16)[None]
    with jax.named_scope("send_summary"):
        for dy in FAR_FIRST:
            there = row_at(dy, 0)
            for dx in FAR_FIRST:
                for dz in FAR_FIRST:
                    if dy or dx or dz:
                        pltpu.make_async_remote_copy(
                            src_ref=sums_buf.at[mine],
                            dst_ref=sums_buf.at[mine],
                            send_sem=sum_send,
                            recv_sem=sum_recv.at[dy],
                            device_id=(there, xs[dx] + zs[dz]),
                            device_id_type=MESH,
                        ).start()

    low = lax.broadcasted_iota(jnp.int32, (T, 128), 1) < HD

    with jax.named_scope("query"):
        query = dot(members, wq[...]).astype(BF16)
    with jax.named_scope("attend"):
        square = jnp.zeros((T, 128), F32)
        for j in range(PAIRS):
            at = slice(j * 128, (j + 1) * 128)
            got = attend_pair(query[:, at], key[:, at], value[:, at], low)
            square = square + got * got
            att[:, at] = got
        scale = lax.rsqrt(jnp.sum(square, axis=1, keepdims=True) / D + 1e-6)
        branch = (att[...] * scale * gain_c_ref[...]).astype(BF16)
        branch = dot(branch, wo[...]).astype(BF16)
    with jax.named_scope("pack_back"):
        for j in range(PAIRS):
            stage[pl.ds(j, ROWS, stride=8), :] = dot(scatter, branch[:, j * 128 : (j + 1) * 128])
        back_buf[...] = stage[...].astype(BF16).reshape(N, 16, 128)
    with jax.named_scope("send_back"):
        to_all(back_buf, home_buf, back_send, back_recv, -1)

    with jax.named_scope("pass_summary"):
        passes = []
        for dy in FAR_FIRST:
            wait_for(sums_buf, GY - 1 if dy == 0 else GY, sum_recv.at[dy])
            block = sums_buf.at[pl.ds(core * CHIPS + lax.rem(y + 4 - dy, 4) * GY, GY)]
            passes.append(
                pltpu.make_async_remote_copy(
                    src_ref=block,
                    dst_ref=block,
                    send_sem=pass_send.at[dy],
                    recv_sem=pass_recv.at[dy],
                    device_id=(gx + 1 - 2 * core, gy),
                    device_id_type=MESH,
                )
            )
            passes[-1].start()
        for one in passes:
            one.wait()
    with jax.named_scope("attend_summary"):
        stage[...] = sums_buf[...].astype(F32).reshape(N * 16, 128)
        square = jnp.zeros((T, 128), F32)
        for j in range(PAIRS):
            at = slice(j * 128, (j + 1) * 128)
            got = attend_pair(
                q_loc[:, at],
                stage[pl.ds(j, N, stride=16), :].astype(BF16),
                stage[pl.ds(8 + j, N, stride=16), :].astype(BF16),
                low,
            )
            square = square + got * got
            att[:, at] = got
        scale = lax.rsqrt(jnp.sum(square, axis=1, keepdims=True) / D + 1e-6)
        summary = (att[...] * scale * gain_s_ref[...]).astype(BF16)
        att[...] = dot(summary, wo[...])

    with jax.named_scope("mix_out"):
        unpack(home_buf, back_recv)
        pick_back = (iota((T, ROWS), 1) == place_col).astype(BF16)
        mixture = (dot(pick_back, rows[...]) + att[...]).astype(BF16)
        out_ref[...] = mixture

    with jax.named_scope("drain"):
        wait_all(send_buf, fwd_send)
        wait_for(sums_buf, CHIPS - 1, sum_send)
        wait_all(back_buf, back_send)


def body(
    tokens_in, dest_slot, w_query, w_key, w_value, surrogate, gain_cluster, gain_summary, w_out
):
    vmem, hbm = pl.BlockSpec(memory_space=pltpu.VMEM), pl.BlockSpec(memory_space=pl.ANY)
    tiles = pltpu.VMEM((N, 16, 128), BF16)
    weight = pltpu.VMEM((D, D), BF16)
    dma = pltpu.SemaphoreType.DMA
    layer_out = pl.pallas_call(
        kernel,
        out_shape=jax.ShapeDtypeStruct((T, D), BF16),
        in_specs=[hbm] * 9,
        out_specs=vmem,
        scratch_shapes=[
            pltpu.VMEM((T, D), BF16),
            pltpu.VMEM((1, T), jnp.int32),
            pltpu.VMEM((PAIRS, 128), BF16),
            pltpu.VMEM((1, D), F32),
            pltpu.VMEM((1, D), F32),
        ]
        + [weight] * 4
        + [
            pltpu.VMEM((ROWS * 8, 128), F32),
            pltpu.VMEM((ROWS, D), BF16),
            tiles, tiles, tiles, tiles,
            tiles,
            pltpu.VMEM((T, D), F32),
            pltpu.VMEM((T, D), BF16),
            dma((2,)), dma((7,)), dma, dma((GX,)), dma, dma((4,)), dma((4,)), dma((4,)), dma, dma((GX,)),
        ],
        compiler_params=pltpu.CompilerParams(
            collective_id=0, has_side_effects=True, vmem_limit_bytes=40 * 2**20
        ),
    )(
        *(
            pltpu.with_memory_space_constraint(arg, pltpu.HBM)
            for arg in (
                tokens_in,
                dest_slot.reshape(1, T),
                surrogate.reshape(PAIRS, 128),
                gain_cluster.reshape(1, D),
                gain_summary.reshape(1, D),
                w_query, w_key, w_value, w_out,
            )
        )
    )
    return layer_out


def solution(mesh):
    in_specs = (P(("gx", "gy"), None), P(("gx", "gy")), P(), P(), P(), P(), P(), P(), P())
    out_specs = P(("gx", "gy"), None)
    return jax.shard_map(body, mesh=mesh, in_specs=in_specs, out_specs=out_specs, check_vma=False)
```
